256 devices in a mesh: blk: 8 (over x_lo, y), grp: 32 (over x_hi, z, core).
Axes of the slice: x: 4 (x_hi: 2, x_lo: 2; x = x_hi * 2 + x_lo), y: 4, z: 8, core: 2. Of those that a mesh axis runs over, the one named last changes fastest.
Arguments:
- picture_vectors_prenorm: float32 [4096, 1152], P(('blk', 'grp')), may hold values from -2 to 2, as said below
- caption_vectors_prenorm: float32 [4096, 1152], P(('blk', 'grp')), may hold values from -2 to 2, as said below
- matched_caption_ids: int32 [4096], P(('blk', 'grp')), may hold values from 0 to 4095, each once
- sharpness_coefficient: float32 [1], replicated, may hold values from 4 to 12
- additive_offset_term: float32 [1], replicated, may hold values from -6 to -2
- heads_mixed_concluding: bfloat16 [98304, 1536], P(('blk', 'grp')), may hold values from -6 to 6
- dense_result_adjoint: bfloat16 [98304, 1536], P(('blk', 'grp')), may hold values from -6 to 6
- dense_mapping_matrix: bfloat16 [1536, 1536], P('grp'), may hold values from -0.15625 to 0.15625
Outputs:
- image_grad: float32 [4096, 1152], P(('blk', 'grp'))
- text_grad: float32 [4096, 1152], P(('blk', 'grp'))
- attn_grad: bfloat16 [98304, 1536], P(('blk', 'grp'))
- weight_grad: float32 [1536, 1536], P('grp')
The draws below stay inside these ranges and needn't reach their ends.
Inputs may be any that keep to these rules, and one draw needn't show every extreme that they name: `matched_caption_ids`: each text index appears once. `picture_vectors_prenorm`: raw embedding entries. `caption_vectors_prenorm`: raw embedding entries.
All inputs are finite; a program needn't handle non-finite values.
Results may differ from the reference program's by a relative error of at most 0.0053.
Values may be sent and summed in bfloat16 or wider, within the bound.
No kernel may reach another device: no remote copies, remote signals or barrier semaphores. Data moves between devices by JAX's collectives and lax.ppermute only.
A program may use at most 128 MiB of HBM per device.

```python
import math
import jax
import jax.numpy as jnp
from jax import lax

EMB = 1152
D = 1536
TOK_DEV = 384
PAIRS = 4096
TOKENS = 98304
DEVICES = 256


def draw_picture_vectors_prenorm(key, part):
    key = jax.random.fold_in(key, 17)
    scale_key, entry_key = jax.random.split(key)
    scales = jnp.exp(jax.random.uniform(scale_key, (PAIRS, 1), jnp.float32, math.log(0.3), math.log(3.0)))
    entries = jnp.clip(jax.random.normal(entry_key, (PAIRS, EMB), jnp.float32), -5.0, 5.0)
    return entries * scales / math.sqrt(EMB)


def draw_caption_vectors_prenorm(key, part):
    key = jax.random.fold_in(key, 29)
    scale_key, entry_key = jax.random.split(key)
    scales = jnp.exp(jax.random.uniform(scale_key, (PAIRS, 1), jnp.float32, math.log(0.3), math.log(3.0)))
    entries = jnp.clip(jax.random.normal(entry_key, (PAIRS, EMB), jnp.float32), -5.0, 5.0)
    return entries * scales / math.sqrt(EMB)


def shard_levels(key, shape, pieces, low, top_value):
    def one(dim, blocks):
        heights = jax.random.uniform(jax.random.fold_in(jax.random.fold_in(key, 6), dim), (blocks,), jnp.float32, low / len(pieces), top_value / len(pieces))
        return jnp.repeat(jnp.exp(heights), shape[dim] // blocks).reshape((-1,) + (1,) * (len(shape) - dim - 1))

    level = one(*pieces[0])
    for cut in pieces[1:]:
        level = level * one(*cut)
    return level


def bell_draw(own_key, shape, scale, limit, pieces=(), dtype=jnp.bfloat16):
    factor_of = shard_levels(own_key, shape, pieces, -0.22, 0.18) if pieces else 1.0
    values = jax.random.normal(own_key, shape, jnp.float32) * scale * factor_of
    return jnp.minimum(jnp.maximum(values, -limit), limit).astype(dtype)


def setup_inputs(seed: int = 0) -> dict:
    splits = jax.random.split(jax.random.key(seed), 9)
    picture_vectors_prenorm = draw_picture_vectors_prenorm(jax.random.fold_in(splits[8], 71), 0)
    caption_vectors_prenorm = draw_caption_vectors_prenorm(jax.random.fold_in(splits[8], 71), 0)
    matched_caption_ids = jax.random.permutation(splits[2], PAIRS).astype(jnp.int32)
    sharpness_coefficient = jnp.clip(jax.random.uniform(splits[3], (1,), jnp.float32, 4.0, 12.0), 4.0, 12.0)
    additive_offset_term = jnp.clip(jax.random.uniform(splits[4], (1,), jnp.float32, -6.0, -2.0), -6.0, -2.0)
    heads_mixed_concluding = bell_draw(splits[5], (TOKENS, D), 1.0, 6.0, ((0, 256),))
    dense_result_adjoint = bell_draw(splits[6], (TOKENS, D), 1.0, 6.0, ((0, 256),))
    dense_mapping_matrix = bell_draw(splits[7], (D, D), D ** -0.5, 0.15625, ((0, 32),))
    return dict(picture_vectors_prenorm=picture_vectors_prenorm, caption_vectors_prenorm=caption_vectors_prenorm, matched_caption_ids=matched_caption_ids, sharpness_coefficient=sharpness_coefficient, additive_offset_term=additive_offset_term, heads_mixed_concluding=heads_mixed_concluding, dense_result_adjoint=dense_result_adjoint, dense_mapping_matrix=dense_mapping_matrix)


stability_floor = 1e-06

def unit_rows(raw):
    row_scale = lax.rsqrt(lax.optimization_barrier(jnp.sum(raw * raw, axis=1, keepdims=True)) + stability_floor)
    return (raw * row_scale, row_scale)

def back_through_norm(normed, row_scale, row_grad):
    along_unit = lax.optimization_barrier(jnp.sum(normed * row_grad, axis=1, keepdims=True))
    return (row_grad - normed * along_unit) * row_scale

def weighted_sum(query_half, key_half, labels, sigmoid_multiplier, bias_value):
    inner_dots = lax.dot_general(query_half, key_half, (((1,), (1,)), ((), ())), preferred_element_type=jnp.float32)
    logits = sigmoid_multiplier * inner_dots + bias_value
    pair_weights = (sigmoid_multiplier * (jax.nn.sigmoid(logits) - labels)).astype(jnp.bfloat16)
    return jnp.dot(pair_weights, key_half, preferred_element_type=jnp.float32)

def reference(picture_vectors_prenorm, caption_vectors_prenorm, matched_caption_ids, sharpness_coefficient, additive_offset_term, heads_mixed_concluding, dense_result_adjoint, dense_mapping_matrix):
    image_units, image_scale = unit_rows(picture_vectors_prenorm)
    text_units, text_scale = unit_rows(caption_vectors_prenorm)
    image_half = image_units.astype(jnp.bfloat16)
    text_half = text_units.astype(jnp.bfloat16)
    sigmoid_multiplier = sharpness_coefficient[0]
    bias_value = additive_offset_term[0]
    columns = lax.broadcasted_iota(jnp.int32, (1, PAIRS), 1)
    labels = (matched_caption_ids.astype(jnp.int32)[:, None] == columns).astype(jnp.float32)
    image_unit_grad = weighted_sum(image_half, text_half, labels, sigmoid_multiplier, bias_value)
    text_unit_grad = weighted_sum(text_half, image_half, labels.T, sigmoid_multiplier, bias_value)
    image_grad = back_through_norm(image_units, image_scale, image_unit_grad)
    text_grad = back_through_norm(text_units, text_scale, text_unit_grad)
    attn_grad = lax.dot_general(dense_result_adjoint, dense_mapping_matrix, (((1,), (1,)), ((), ())), preferred_element_type=jnp.float32).astype(jnp.bfloat16)
    attention_block_list = heads_mixed_concluding.reshape(DEVICES, TOK_DEV, D)
    grad_blocks = dense_result_adjoint.reshape(DEVICES, TOK_DEV, D)

    def add_device(total, blocks):
        term = lax.dot_general(blocks[0], blocks[1], (((0,), (0,)), ((), ())), preferred_element_type=jnp.float32)
        return (total + term, None)
    weight_sum, unused = lax.scan(add_device, jnp.zeros((D, D), jnp.float32), (attention_block_list, grad_blocks))
    weight_grad = weight_sum * (1.0 / math.sqrt(TOKENS))
    return (image_grad, text_grad, attn_grad, weight_grad)
```

```python
import math

import jax
import jax.numpy as jnp
from jax import lax
from jax.sharding import Mesh, PartitionSpec as P

stability_floor = 1e-06

AXES = ("xl", "y", "xh", "z", "c")
SIZES = (2, 4, 2, 8, 2)
PLANE = ("y", "xh", "xl")


def unit_rows(raw):
    row_scale = lax.rsqrt(jnp.sum(raw * raw, axis=1, keepdims=True) + stability_floor)
    return (raw * row_scale, row_scale)


def back_through_norm(normed, row_scale, row_grad):
    along_unit = jnp.sum(normed * row_grad, axis=1, keepdims=True)
    return (row_grad - normed * along_unit) * row_scale


def swap_cores(x):
    return lax.ppermute(x, "c", [(0, 1), (1, 0)])


def exchange(x, axes):
    return lax.all_to_all(x, axes, 0, 0, tiled=True)


def to_everyone(x, count):
    return jnp.broadcast_to(x[None], (count,) + x.shape)


def fold(x):
    lead, rows = x.shape[:-2], x.shape[-2]
    return jnp.swapaxes(x.reshape(lead + (rows, 3, 384)), -3, -2).reshape(lead + (3 * rows, 384))


def unfold(x):
    lead, rows = x.shape[:-2], x.shape[-2] // 3
    return jnp.swapaxes(x.reshape(lead + (3, rows, 384)), -3, -2).reshape(lead + (rows, 1152))


def per_device(
    picture_vectors_prenorm,
    caption_vectors_prenorm,
    matched_caption_ids,
    sharpness_coefficient,
    additive_offset_term,
    heads_mixed_concluding,
    dense_result_adjoint,
    dense_mapping_matrix,
):
    f32, bf16 = jnp.float32, jnp.bfloat16
    xl, y, xh, c = (lax.axis_index(name) for name in ("xl", "y", "xh", "c"))
    other_tokens = swap_cores(heads_mixed_concluding)
    other_adjoint = swap_cores(dense_result_adjoint)

    image_units, image_scale = unit_rows(picture_vectors_prenorm)
    text_units, text_scale = unit_rows(caption_vectors_prenorm)
    image_half = image_units.astype(bf16)
    text_half = text_units.astype(bf16)

    own_piece = lax.dynamic_slice(dense_mapping_matrix, (xl * 24, y * 384), (24, 384))
    sent = jnp.concatenate([text_half, unfold(own_piece)], axis=0)
    along_z = exchange(to_everyone(sent, 8), "z")
    text_here = along_z[:, :16].reshape(128, 1152)
    mapping_piece = fold(along_z[:, 16:]).reshape(192, 384)
    text_block = jnp.concatenate([text_here, swap_cores(text_here)], axis=0)

    def own_columns(tokens):
        blocks = tokens.T.reshape(16, 2, 48, 384)
        return lax.dynamic_index_in_dim(blocks, c, 1, keepdims=False).reshape(768, 384)

    weight_share = jnp.dot(
        jnp.concatenate([own_columns(heads_mixed_concluding), own_columns(other_tokens)], axis=1),
        jnp.concatenate([dense_result_adjoint, other_adjoint], axis=0),
        preferred_element_type=f32,
    ).astype(bf16)
    weight_share = weight_share.reshape(2, 8, 2, 24, 4, 384).transpose(4, 0, 2, 1, 3, 5)
    weight_share = weight_share.reshape(16, 192, 384)
    id_parts = jnp.stack([matched_caption_ids // 64, matched_caption_ids % 64]).astype(bf16)
    id_rows = jnp.pad(id_parts, ((0, 6), (0, 368)))
    image_sent = jnp.concatenate([fold(image_half), id_rows], axis=0)
    in_plane = exchange(
        jnp.concatenate([weight_share, to_everyone(image_sent, 16)], axis=1), PLANE
    )
    weight_plane = jnp.sum(in_plane[:, :192].astype(f32), axis=0)
    image_block = unfold(in_plane[:, 192:240]).reshape(256, 1152)
    ids = in_plane[:, 240:242, :16].astype(jnp.int32)
    ids = (ids[:, 0] * 64 + ids[:, 1]).reshape(256, 1)

    sharpness = sharpness_coefficient[0]
    offset = additive_offset_term[0]
    plane_first = ((xl * 4 + y) * 2 + xh) * 256
    row = lax.broadcasted_iota(jnp.int32, (1, 256), 1)
    core = jnp.where(row < 128, c, 1 - c)
    row = row % 128
    text_index = plane_first + ((row // 16) * 2 + core) * 16 + row % 16
    dots = lax.dot_general(
        image_block, text_block, (((1,), (1,)), ((), ())), preferred_element_type=f32
    )
    labels = (ids == text_index).astype(f32)
    pair_weights = (sharpness * (jax.nn.sigmoid(sharpness * dots + offset) - labels)).astype(bf16)
    image_part = jnp.dot(pair_weights, text_block, preferred_element_type=f32).astype(bf16)
    text_part = lax.dot_general(
        pair_weights, image_block, (((0,), (0,)), ((), ())), preferred_element_type=f32
    )
    text_part = text_part[:128] + swap_cores(text_part[128:].astype(bf16)).astype(f32)

    back = jnp.concatenate(
        [
            text_part.astype(bf16).reshape(8, 16, 1152),
            unfold(weight_plane.astype(bf16).reshape(8, 24, 384)),
        ],
        axis=1,
    )
    back = jnp.sum(exchange(back, "z").astype(f32), axis=0)
    text_grad = back_through_norm(text_units, text_scale, back[:16])
    weight_piece = fold(back[16:]) * (1.0 / math.sqrt(98304))
    pieces = exchange(to_everyone(weight_piece, 8), ("xl", "y"))
    weight_grad = pieces.reshape(2, 4, 24, 384).transpose(0, 2, 1, 3).reshape(48, 1536)

    back = jnp.concatenate(
        [fold(image_part.reshape(16, 16, 1152)), to_everyone(mapping_piece, 16)], axis=1
    )
    back = exchange(back, PLANE)
    image_grad = back_through_norm(
        image_units, image_scale, unfold(jnp.sum(back[:, :48].astype(f32), axis=0))
    )
    rows = back[:, 48:].reshape(4, 2, 2, 8, 24, 384).transpose(1, 3, 2, 4, 0, 5)
    rows = rows.reshape(16, 48, 1536)
    other_rows = swap_cores(rows)
    mapping = jnp.stack(
        [jnp.where(c == 0, rows, other_rows), jnp.where(c == 0, other_rows, rows)], axis=1
    ).reshape(1536, 1536)
    attn_grad = lax.dot_general(
        dense_result_adjoint, mapping, (((1,), (1,)), ((), ())), preferred_element_type=f32
    ).astype(bf16)
    return (image_grad, text_grad, attn_grad, weight_grad)


def solution(mesh):
    chips = Mesh(mesh.devices.reshape(SIZES), AXES)
    everywhere = P(AXES, None)
    by_group = P(("xh", "z", "c"), None)
    return jax.shard_map(
        per_device,
        mesh=chips,
        in_specs=(
            everywhere,
            everywhere,
            P(AXES),
            P(),
            P(),
            everywhere,
            everywhere,
            by_group,
        ),
        out_specs=(everywhere, everywhere, everywhere, by_group),
        check_vma=False,
    )
```

```python
import math

import jax
import jax.numpy as jnp
from jax import lax
from jax.sharding import Mesh, PartitionSpec as P

stability_floor = 1e-06

AXES = ("xl", "y", "xh", "z", "c")
SIZES = (2, 4, 2, 8, 2)
ROW = (("xl", "xh"), (0, 2, 1, 3))
COLUMN = ("y", (0, 1, 2, 3))


def unit_rows(raw):
    row_scale = lax.rsqrt(jnp.sum(raw * raw, axis=1, keepdims=True) + stability_floor)
    return (raw * row_scale, row_scale)


def back_through_norm(normed, row_scale, row_grad):
    along_unit = jnp.sum(normed * row_grad, axis=1, keepdims=True)
    return (row_grad - normed * along_unit) * row_scale


def swap_cores(x):
    return lax.ppermute(x, "c", [(0, 1), (1, 0)])


def turn(x, ring, by):
    axes, at = ring
    return lax.ppermute(x, axes, [(at[i], at[(i + by) % 4]) for i in range(4)])


def swap_halves(x):
    axes, at = ROW
    return lax.ppermute(x, axes, [(at[i], at[3 - i]) for i in range(4)])


def exchange(x, axes):
    return lax.all_to_all(x, axes, 0, 0, tiled=True)


def to_everyone(x, count):
    return jnp.broadcast_to(x[None], (count,) + x.shape)


def fold(x):
    lead, rows = x.shape[:-2], x.shape[-2]
    return jnp.swapaxes(x.reshape(lead + (rows, 3, 384)), -3, -2).reshape(lead + (3 * rows, 384))


def unfold(x):
    lead, rows = x.shape[:-2], x.shape[-2] // 3
    return jnp.swapaxes(x.reshape(lead + (3, rows, 384)), -3, -2).reshape(lead + (rows, 1152))


def gathered(x, ring):
    return [x] + [turn(x, ring, k) for k in (1, 2, 3)]


def summed_back(parts, ring):
    total = parts[0].astype(jnp.float32)
    for k in (1, 2, 3):
        total = total + turn(parts[k], ring, -k).astype(jnp.float32)
    return total


def per_device(
    picture_vectors_prenorm,
    caption_vectors_prenorm,
    matched_caption_ids,
    sharpness_coefficient,
    additive_offset_term,
    heads_mixed_concluding,
    dense_result_adjoint,
    dense_mapping_matrix,
):
    f32, bf16 = jnp.float32, jnp.bfloat16
    xl, y, xh, c = (lax.axis_index(name) for name in ("xl", "y", "xh", "c"))

    def columns_of(core):
        blocks = heads_mixed_concluding.T.reshape(16, 2, 48, 384)
        return lax.dynamic_index_in_dim(blocks, core, 1, keepdims=False).reshape(768, 384)

    other_adjoint = swap_cores(dense_result_adjoint)
    other_tokens = swap_cores(columns_of(1 - c))

    image_units, image_scale = unit_rows(picture_vectors_prenorm)
    text_units, text_scale = unit_rows(caption_vectors_prenorm)
    image_half = image_units.astype(bf16)
    text_half = text_units.astype(bf16)

    own_piece = lax.dynamic_slice(dense_mapping_matrix, (0, y * 384), (48, 384))
    sent = jnp.concatenate([fold(text_half), own_piece], axis=0)
    along_z = exchange(to_everyone(sent, 8), "z")
    text_here = unfold(along_z[:, :48]).reshape(128, 1152)
    mapping_piece = along_z[:, 48:]
    text_block = jnp.concatenate([text_here, swap_cores(text_here)], axis=0)

    id_parts = jnp.stack([matched_caption_ids // 64, matched_caption_ids % 64]).astype(bf16)
    id_rows = jnp.pad(id_parts, ((0, 6), (0, 1152 - 16)))
    image_sent = jnp.concatenate([image_half, id_rows], axis=0)
    column = jnp.stack(gathered(image_sent, COLUMN))
    image_sent = jnp.concatenate(gathered(column, ROW))
    image_block = image_sent[:, :16].reshape(256, 1152)
    ids = image_sent[:, 16:18, :16].astype(jnp.int32)
    ids = (ids[:, 0] * 64 + ids[:, 1]).reshape(256, 1)

    weight_share = jnp.dot(
        jnp.concatenate([columns_of(c), other_tokens], axis=1),
        jnp.concatenate([dense_result_adjoint, other_adjoint], axis=0),
        preferred_element_type=f32,
    ).astype(bf16)
    weight_share = weight_share.reshape(2, 8, 48, 1536)

    def column_block(share, k):
        return lax.dynamic_slice_in_dim(share, ((y + 4 - k) % 4) * 384, 384, axis=-1)

    def half_of(share, which):
        return lax.dynamic_index_in_dim(share, which, 0, keepdims=False)

    first = summed_back([column_block(weight_share[:, :4], k) for k in range(4)], COLUMN)
    first = half_of(first, xh) + swap_halves(half_of(first, 1 - xh).astype(bf16)).astype(f32)
    second = weight_share[:, 4:]
    second = half_of(second, xh).astype(f32) + swap_halves(half_of(second, 1 - xh)).astype(f32)
    second = second.astype(bf16)
    second = summed_back([column_block(second, k) for k in range(4)], COLUMN)
    weight_plane = jnp.concatenate([first, second], axis=0).astype(bf16)

    sharpness = sharpness_coefficient[0]
    offset = additive_offset_term[0]
    plane_first = ((xl * 4 + y) * 2 + xh) * 256
    row = lax.broadcasted_iota(jnp.int32, (1, 256), 1)
    core = jnp.where(row < 128, c, 1 - c)
    row = row % 128
    text_index = plane_first + ((row // 16) * 2 + core) * 16 + row % 16
    dots = lax.dot_general(
        image_block, text_block, (((1,), (1,)), ((), ())), preferred_element_type=f32
    )
    labels = (ids == text_index).astype(f32)
    pair_weights = (sharpness * (jax.nn.sigmoid(sharpness * dots + offset) - labels)).astype(bf16)
    image_part = jnp.dot(pair_weights, text_block, preferred_element_type=f32).astype(bf16)
    text_part = lax.dot_general(
        pair_weights, image_block, (((0,), (0,)), ((), ())), preferred_element_type=f32
    )
    text_part = text_part[:128] + swap_cores(text_part[128:].astype(bf16)).astype(f32)

    image_part = image_part.reshape(4, 64, 1152)
    image_part = summed_back([image_part[k] for k in range(4)], ROW).astype(bf16)
    image_part = image_part.reshape(4, 16, 1152)
    image_part = summed_back([image_part[k] for k in range(4)], COLUMN)
    image_grad = back_through_norm(image_units, image_scale, image_part)

    back = jnp.concatenate([fold(text_part.astype(bf16).reshape(8, 16, 1152)), weight_plane], 1)
    back = jnp.sum(exchange(back, "z").astype(f32), axis=0)
    text_grad = back_through_norm(text_units, text_scale, unfold(back[:48]))
    weight_piece = back[48:] * (1.0 / math.sqrt(98304))
    pieces = exchange(to_everyone(weight_piece.astype(bf16), 8), ("xl", "y"))
    weight_grad = jnp.sum(pieces.reshape(2, 4, 48, 384).astype(f32), axis=0)
    weight_grad = weight_grad.transpose(1, 0, 2).reshape(48, 1536)

    def both_halves(x):
        other = swap_halves(x)
        low = xh == 0
        return jnp.stack([jnp.where(low, x, other), jnp.where(low, other, x)])

    first = jnp.concatenate(gathered(both_halves(mapping_piece[:4]), COLUMN), axis=-1)
    second = jnp.concatenate(gathered(mapping_piece[4:], COLUMN), axis=-1)
    second = both_halves(second)

    def both_cores(x):
        other = swap_cores(x)
        low = c == 0
        return jnp.stack([jnp.where(low, x, other), jnp.where(low, other, x)], axis=2)

    mapping = jnp.concatenate([both_cores(first), both_cores(second)], axis=1).reshape(1536, 1536)
    adjoint = jnp.concatenate([column_block(dense_result_adjoint, k) for k in range(4)], axis=1)
    attn_grad = lax.dot_general(
        adjoint, mapping, (((1,), (1,)), ((), ())), preferred_element_type=f32
    ).astype(bf16)
    return (image_grad, text_grad, attn_grad, weight_grad)


def solution(mesh):
    chips = Mesh(mesh.devices.reshape(SIZES), AXES)
    everywhere = P(AXES, None)
    by_group = P(("xh", "z", "c"), None)
    return jax.shard_map(
        per_device,
        mesh=chips,
        in_specs=(
            everywhere,
            everywhere,
            P(AXES),
            P(),
            P(),
            everywhere,
            everywhere,
            by_group,
        ),
        out_specs=(everywhere, everywhere, everywhere, by_group),
        check_vma=False,
    )
```

```python
import math

import jax
import jax.numpy as jnp
from jax import lax
from jax.experimental import pallas as pl
from jax.experimental.pallas import tpu as pltpu
from jax.sharding import Mesh, PartitionSpec as P

stability_floor = 1e-06
f32, bf16 = jnp.float32, jnp.bfloat16

AXES = ("xl", "y", "xh", "z", "c")
SIZES = (2, 4, 2, 8, 2)
ROW = (("xl", "xh"), (0, 2, 1, 3))
COLUMN = ("y", (0, 1, 2, 3))
CUT = 144
BACK = (((1,), (1,)), ((), ()))


def swap_cores(x):
    return lax.ppermute(x, "c", [(0, 1), (1, 0)])


def turn(x, ring, by):
    axes, at = ring
    return lax.ppermute(x, axes, [(at[i], at[(i + by) % 4]) for i in range(4)])


def swap_halves(x):
    axes, at = ROW
    return lax.ppermute(x, axes, [(at[i], at[3 - i]) for i in range(4)])


def swap_pairs(x):
    return lax.ppermute(x, "xl", [(0, 1), (1, 0)])


def swap_far(x):
    return lax.ppermute(x, "xh", [(0, 1), (1, 0)])


def exchange(x, axes):
    return lax.all_to_all(x, axes, 0, 0, tiled=True)


def after(x, *earlier):
    return lax.optimization_barrier((x, *earlier))[0]


def fold(x):
    return jnp.concatenate([x[:, i * 384 : (i + 1) * 384] for i in range(3)], axis=0)


def unfold(x):
    return jnp.concatenate([x[i * 16 : (i + 1) * 16] for i in range(3)], axis=1)


def unit_rows(raw):
    row_scale = lax.rsqrt(jnp.sum(raw * raw, axis=1, keepdims=True) + stability_floor)
    return raw * row_scale, row_scale


def back_through_norm(raw, row_grad):
    normed, row_scale = unit_rows(raw)
    along_unit = jnp.sum(normed * row_grad, axis=1, keepdims=True)
    return (row_grad - normed * along_unit) * row_scale


def call(kernel, outs, place, *operands, scratch=(), flops=0, spaces=()):
    moved = sum(math.prod(o.shape) * o.dtype.itemsize for o in (*outs, *operands))
    spaces = tuple(spaces) + (pltpu.VMEM,) * (len(operands) - len(spaces))
    return pl.pallas_call(
        kernel,
        out_shape=tuple(outs),
        in_specs=[pl.BlockSpec(memory_space=space) for space in (pltpu.SMEM, *spaces)],
        out_specs=tuple(pl.BlockSpec(memory_space=pltpu.VMEM) for _ in outs),
        scratch_shapes=scratch,
        compiler_params=pltpu.CompilerParams(vmem_limit_bytes=16 * 2**20),
        cost_estimate=pl.CostEstimate(flops=flops, bytes_accessed=moved, transcendentals=0),
    )(place, *operands)


def shape(*dims, dtype=bf16):
    return jax.ShapeDtypeStruct(dims, dtype)


def text_kernel(place, cap, rows, z_out):
    text = fold(unit_rows(cap[...])[0].astype(bf16))
    for k in range(8):
        z_out[k, :48, :] = text
        for j in range(4):
            z_out[k, 48 + j * 48 : 96 + j * 48, :] = rows[:, j * 384 : j * 384 + 384]


def weight_kernel(place, ids, pic, tokens, other_tokens, adj, other_adj, *rest):
    a0, a1, a2, a3, b_own, b_out, image, turned, own, other = rest
    y, low, c = place[0], place[2] == 0, place[3]
    line = lax.broadcasted_iota(jnp.int32, (16, 384), 0)
    number = jnp.zeros((16, 384), jnp.int32)
    for i in range(16):
        number = jnp.where(line == i, ids[i], number)
    lane = lax.broadcasted_iota(jnp.int32, (16, 384), 1)
    split = jnp.where(lane == 0, number >> 6, jnp.where(lane == 1, number & 63, 0))
    image[48:, :] = split.astype(f32).astype(bf16)
    image[:48, :] = fold(unit_rows(pic[...])[0].astype(bf16))
    for source, target in ((tokens, own), (other_tokens, other)):
        turned[...] = source[...].T
        for chip in range(16):
            here = pl.ds(pl.multiple_of(chip * 96 + c * 48, 16), 48)
            target[chip * 48 : chip * 48 + 48, :] = turned[here, :]
    for k, out in enumerate((a0, a1, a2, a3)):
        at = pl.ds(pl.multiple_of(((y - k) & 3) * 384, 384), 384)
        acc = jnp.dot(own[...], adj[:, at], preferred_element_type=f32)
        acc = acc + jnp.dot(other[...], other_adj[:, at], preferred_element_type=f32)
        acc = acc.astype(bf16)
        out[:CUT, :] = acc[:CUT]
        out[CUT : 2 * CUT, :] = acc[384 : 384 + CUT]
        b_own[:, at] = jnp.where(low, acc[CUT:384], acc[384 + CUT :])
        b_out[:, at] = jnp.where(low, acc[384 + CUT :], acc[CUT:384])
        if k:
            out[2 * CUT :, :] = image[...]


def first_sum_kernel(
    place, a0, a1, a2, a3, b_own, b_in, image, a_own, near, b0, b1, b2, b3, total
):
    y, xh = place[0], place[2]
    total[...] = a0[...].astype(f32)
    for part in (a1, a2, a3):
        total[...] += part[: 2 * CUT, :].astype(f32)
    a_own[...] = total[pl.ds(pl.multiple_of(xh * CUT, 16), CUT), :]
    near[:CUT, :] = total[pl.ds(pl.multiple_of((1 - xh) * CUT, 16), CUT), :].astype(bf16)
    for k, out in enumerate((b0, b1, b2, b3)):
        at = pl.ds(pl.multiple_of(((y - k) & 3) * 384, 384), 384)
        both = b_own[:, at].astype(f32) + b_in[:, at].astype(f32)
        out[...] = both.astype(out.dtype)
    near[CUT : CUT + 64, :] = image[...]
    for k, part in enumerate((a1, a2, a3)):
        near[CUT + 64 + 64 * k : CUT + 128 + 64 * k, :] = part[2 * CUT :, :]


def second_sum_kernel(place, a_own, near_in, b0, b1, b2, b3, out):
    out[:CUT, :] = (a_own[...] + near_in[:CUT, :].astype(f32)).astype(bf16)
    total = b0[...]
    for part in (b1, b2, b3):
        total = total + part[...].astype(f32)
    out[CUT:, :] = total.astype(bf16)


def tile_kernel(
    place, knobs, i0, i1, i2, i3, text, other_text, g0, g1, g2, g3, t_own, t_out, images, texts, ids
):
    y, xl, xh, c = place[0], place[1], place[2], place[3]
    for k, part in enumerate((i0, i1, i2, i3)):
        first = part.shape[0] - 256
        for j in range(4):
            at = k * 64 + j * 16
            here = first + j * 64
            images[at : at + 16, :] = unfold(part[here : here + 48, :])
            split = part[here + 48 : here + 64, :128].astype(f32)
            ids[at : at + 16, :] = (split[:, 0:1] * 64.0 + split[:, 1:2]).astype(jnp.int32)
    for k in range(8):
        texts[k * 16 : k * 16 + 16, :] = unfold(text[k, :48, :])
        texts[128 + k * 16 : 144 + k * 16, :] = unfold(other_text[k, :, :])
    sharpness, offset = knobs[0, 0], knobs[0, 1]
    col = lax.broadcasted_iota(jnp.int32, (256, 256), 1)
    core = jnp.where(col < 128, c, 1 - c)
    first = ((xl * 4 + y) * 2 + xh) * 256
    index = first + (((col & 127) >> 4) * 2 + core) * 16 + (col & 15)
    dots = lax.dot_general(images[...], texts[...], BACK, preferred_element_type=f32)
    labels = (ids[...] == index).astype(f32)
    weights = sharpness * (jax.nn.sigmoid(sharpness * dots + offset) - labels)
    half = weights.astype(bf16)
    for k, out in enumerate((g0, g1, g2, g3)):
        part = jnp.dot(half[k * 64 : k * 64 + 64], texts[...], preferred_element_type=f32)
        for j in range(4):
            out[j * 48 : j * 48 + 48, :] = fold(part[j * 16 : j * 16 + 16]).astype(out.dtype)
    half = weights.T.astype(bf16)
    t_own[...] = jnp.dot(half[:128], images[...], preferred_element_type=f32)
    t_out[...] = jnp.dot(half[128:], images[...], preferred_element_type=f32).astype(bf16)


def send_back_kernel(place, t_own, t_in, weight, out):
    total = (t_own[...] + t_in[...].astype(f32)).astype(bf16)
    for k in range(8):
        out[k, :48, :] = fold(total[k * 16 : k * 16 + 16])
        out[k, 48:, :] = weight[k * 48 : k * 48 + 48, :]


def text_end_kernel(place, back, cap, grad, pieces):
    total = back[0].astype(f32)
    for k in range(1, 8):
        total = total + back[k].astype(f32)
    grad[...] = back_through_norm(cap[...], unfold(total[:48]))
    piece = total[48:] * (1.0 / math.sqrt(98304))
    for k in range(8):
        pieces[k] = piece


def image_middle_kernel(place, g0, g1, g2, g3, h0, h1, h2, h3):
    total = g0[...]
    for part in (g1, g2, g3):
        total = total + part[...].astype(f32)
    for k, out in enumerate((h0, h1, h2, h3)):
        out[...] = total[k * 48 : k * 48 + 48].astype(out.dtype)


def image_end_kernel(place, h0, h1, h2, h3, pic, grad):
    total = h0[...]
    for part in (h1, h2, h3):
        total = total + part[...].astype(f32)
    grad[...] = back_through_norm(pic[...], unfold(total))


def weight_end_kernel(place, pieces, grad):
    for k in range(4):
        grad[:, k * 384 : k * 384 + 384] = pieces[k] + pieces[4 + k]


def project_kernel(place, adj, w, other_w, *rest):
    out, rows = rest[-2:]
    c = place[3]
    for z in range(8):
        for k in range(4):
            at = slice(k * 384, k * 384 + 384)
            rows[z * 2 + c, :, at] = w[z, k * 48 : k * 48 + 48, :]
            rows[z * 2 + 1 - c, :, at] = other_w[z, k * 48 : k * 48 + 48, :]
    for k in range(2):
        part = rows[k * 8 : k * 8 + 8].reshape(384, 1536)
        out[:, k * 384 : k * 384 + 384] = lax.dot_general(
            adj[...], part, BACK, preferred_element_type=f32
        ).astype(bf16)


def project(place, half, adj, w, other_w, before=None):
    whole = pl.BlockSpec(memory_space=pltpu.VMEM)
    operands = [adj, w, other_w] + ([] if before is None else [before])
    in_specs = [whole] * 3 + ([] if before is None else [pl.BlockSpec(memory_space=pl.ANY)])
    return pl.pallas_call(
        project_kernel,
        grid_spec=pltpu.PrefetchScalarGridSpec(
            num_scalar_prefetch=1,
            grid=(1,),
            in_specs=in_specs,
            out_specs=pl.BlockSpec((384, 768), lambda i, place: (0, place[half])),
            scratch_shapes=[pltpu.VMEM((16, 48, 1536), bf16)],
        ),
        out_shape=shape(384, 1536),
        input_output_aliases={} if before is None else {4: 0},
        compiler_params=pltpu.CompilerParams(vmem_limit_bytes=16 * 2**20),
        cost_estimate=pl.CostEstimate(
            flops=2 * 384 * 768 * 1536, bytes_accessed=6 * 2**20, transcendentals=0
        ),
    )(place, *operands)


def per_device(
    picture_vectors_prenorm,
    caption_vectors_prenorm,
    matched_caption_ids,
    sharpness_coefficient,
    additive_offset_term,
    heads_mixed_concluding,
    dense_result_adjoint,
    dense_mapping_matrix,
):
    y, xl, xh, c = (lax.axis_index(name) for name in ("y", "xl", "xh", "c"))
    place = jnp.stack([y, xl, xh, c, 1 - xh]).astype(jnp.int32)
    other_adjoint = swap_cores(dense_result_adjoint)
    other_tokens = swap_cores(heads_mixed_concluding)

    (along_z,) = call(
        text_kernel, (shape(8, 240, 384),), place, caption_vectors_prenorm, dense_mapping_matrix
    )
    along_z = exchange(along_z, "z")

    *a, b_own, b_out, image = call(
        weight_kernel,
        (
            shape(2 * CUT, 384),
            *[shape(2 * CUT + 64, 384)] * 3,
            shape(384 - CUT, 1536),
            shape(384 - CUT, 1536),
            shape(64, 384),
        ),
        place,
        matched_caption_ids,
        picture_vectors_prenorm,
        heads_mixed_concluding,
        other_tokens,
        dense_result_adjoint,
        other_adjoint,
        scratch=[
            pltpu.VMEM((1536, 384), bf16),
            pltpu.VMEM((768, 384), bf16),
            pltpu.VMEM((768, 384), bf16),
        ],
        spaces=(pltpu.SMEM,),
        flops=4 * 768 * 384 * 1536,
    )
    b_in = swap_halves(b_out)
    a_in = [turn(a[k], COLUMN, -k) for k in (1, 2, 3)]
    a_own, near, *b = call(
        first_sum_kernel,
        (
            shape(CUT, 384, dtype=f32),
            shape(CUT + 256, 384),
            shape(384 - CUT, 384, dtype=f32),
            *[shape(384 - CUT, 384)] * 3,
        ),
        place,
        a[0],
        *a_in,
        b_own,
        b_in,
        image,
        scratch=[pltpu.VMEM((2 * CUT, 384), f32)],
    )
    near_in = swap_halves(near)
    b = [b[0]] + [turn(b[k], COLUMN, -k) for k in (1, 2, 3)]
    column = near[CUT:]
    images = [column, near_in, swap_pairs(column), swap_far(column)]
    (weight_plane,) = call(second_sum_kernel, (shape(384, 384),), place, a_own, near_in, *b)
    images = [after(image, weight_plane) for image in images]

    along_z = after(along_z, near)
    other_text = swap_cores(along_z[:, :48])
    knobs = jnp.concatenate([sharpness_coefficient, additive_offset_term]).reshape(1, 2)
    *g, t_own, t_out = call(
        tile_kernel,
        (
            shape(192, 384, dtype=f32),
            *[shape(192, 384)] * 3,
            shape(128, 1152, dtype=f32),
            shape(128, 1152),
        ),
        place,
        knobs,
        *images,
        along_z,
        other_text,
        scratch=[
            pltpu.VMEM((256, 1152), bf16),
            pltpu.VMEM((256, 1152), bf16),
            pltpu.VMEM((256, 1), jnp.int32),
        ],
        flops=6 * 256 * 256 * 1152,
    )

    rows = after(along_z[:, 48:], *images[1:])
    far_rows = swap_halves(rows)
    core_rows = swap_cores(rows)

    t_in = swap_cores(t_out)
    (back,) = call(send_back_kernel, (shape(8, 96, 384),), place, t_own, t_in, weight_plane)
    g = [after(part, back) for part in g]
    back = exchange(back, "z")
    g = [g[0], swap_halves(g[1]), swap_pairs(g[2]), swap_far(g[3])]
    far_rows = after(far_rows, *g)
    h = call(
        image_middle_kernel, (shape(48, 384, dtype=f32), *[shape(48, 384)] * 3), place, *g
    )
    attn_grad = project(place, 2, dense_result_adjoint, rows, core_rows)
    back = after(back, attn_grad)
    text_grad, pieces = call(
        text_end_kernel,
        (shape(16, 1152, dtype=f32), shape(8, 48, 384, dtype=f32)),
        place,
        back,
        caption_vectors_prenorm,
    )
    pieces = exchange(pieces, ("xl", "y"))
    h = [h[0]] + [turn(h[k], COLUMN, k) for k in (1, 2, 3)]
    (image_grad,) = call(
        image_end_kernel, (shape(16, 1152, dtype=f32),), place, *h, picture_vectors_prenorm
    )
    attn_grad = project(
        place, 4, dense_result_adjoint, far_rows, swap_cores(far_rows), attn_grad
    )
    pieces = after(pieces, attn_grad, image_grad)
    (weight_grad,) = call(weight_end_kernel, (shape(48, 1536, dtype=f32),), place, pieces)
    return (image_grad, text_grad, attn_grad, weight_grad)


def solution(mesh):
    chips = Mesh(mesh.devices.reshape(SIZES), AXES)
    everywhere = P(AXES, None)
    by_group = P(("xh", "z", "c"), None)
    return jax.shard_map(
        per_device,
        mesh=chips,
        in_specs=(
            everywhere,
            everywhere,
            P(AXES),
            P(),
            P(),
            everywhere,
            everywhere,
            by_group,
        ),
        out_specs=(everywhere, everywhere, everywhere, by_group),
        check_vma=False,
    )
```

```python
import math

import jax
import jax.numpy as jnp
from jax import lax
from jax.experimental import pallas as pl
from jax.experimental.pallas import tpu as pltpu
from jax.sharding import Mesh, PartitionSpec as P

stability_floor = 1e-06
f32, bf16 = jnp.float32, jnp.bfloat16

AXES = ("xl", "y", "xh", "z", "c")
SIZES = (2, 4, 2, 8, 2)
ROW = (("xl", "xh"), (0, 2, 1, 3))
COLUMN = ("y", (0, 1, 2, 3))
CUT = 192
BACK = (((1,), (1,)), ((), ()))


def swap_cores(x):
    return lax.ppermute(x, "c", [(0, 1), (1, 0)])


def turn(x, ring, by):
    axes, at = ring
    return lax.ppermute(x, axes, [(at[i], at[(i + by) % 4]) for i in range(4)])


def swap_halves(x):
    axes, at = ROW
    return lax.ppermute(x, axes, [(at[i], at[3 - i]) for i in range(4)])


def swap_pairs(x):
    return lax.ppermute(x, "xl", [(0, 1), (1, 0)])


def swap_far(x):
    return lax.ppermute(x, "xh", [(0, 1), (1, 0)])


def exchange(x, axes):
    return lax.all_to_all(x, axes, 0, 0, tiled=True)


def after(x, *earlier):
    return lax.optimization_barrier((x, *earlier))[0]


def fold(x):
    return jnp.concatenate([x[:, i * 384 : (i + 1) * 384] for i in range(3)], axis=0)


def unfold(x):
    return jnp.concatenate([x[i * 16 : (i + 1) * 16] for i in range(3)], axis=1)


def unit_rows(raw):
    row_scale = lax.rsqrt(jnp.sum(raw * raw, axis=1, keepdims=True) + stability_floor)
    return raw * row_scale, row_scale


def back_through_norm(raw, row_grad):
    normed, row_scale = unit_rows(raw)
    along_unit = jnp.sum(normed * row_grad, axis=1, keepdims=True)
    return (row_grad - normed * along_unit) * row_scale


def call(kernel, outs, place, *operands, scratch=(), flops=0, spaces=()):
    moved = sum(math.prod(o.shape) * o.dtype.itemsize for o in (*outs, *operands))
    spaces = tuple(spaces) + (pltpu.VMEM,) * (len(operands) - len(spaces))
    return pl.pallas_call(
        kernel,
        out_shape=tuple(outs),
        in_specs=[pl.BlockSpec(memory_space=space) for space in (pltpu.SMEM, *spaces)],
        out_specs=tuple(pl.BlockSpec(memory_space=pltpu.VMEM) for _ in outs),
        scratch_shapes=scratch,
        compiler_params=pltpu.CompilerParams(vmem_limit_bytes=16 * 2**20),
        cost_estimate=pl.CostEstimate(flops=flops, bytes_accessed=moved, transcendentals=0),
    )(place, *operands)


def shape(*dims, dtype=bf16):
    return jax.ShapeDtypeStruct(dims, dtype)


def text_kernel(place, cap, rows, z_out):
    text = fold(unit_rows(cap[...])[0].astype(bf16))
    piece = rows[:, pl.ds(pl.multiple_of(place[1] * 768, 384), 768)]
    for k in range(8):
        z_out[k, :48, :] = text
        z_out[k, 48:96, :] = piece[:, :384]
        z_out[k, 96:, :] = piece[:, 384:]


def weight_kernel(place, ids, pic, tokens, other_tokens, adj, other_adj, *rest):
    a0, a1, a2, a3, b_own, b_out, image, turned, own, other = rest
    y, low, c = place[0], place[2] == 0, place[3]
    line = lax.broadcasted_iota(jnp.int32, (16, 384), 0)
    number = jnp.zeros((16, 384), jnp.int32)
    for i in range(16):
        number = jnp.where(line == i, ids[i], number)
    lane = lax.broadcasted_iota(jnp.int32, (16, 384), 1)
    split = jnp.where(lane == 0, number >> 6, jnp.where(lane == 1, number & 63, 0))
    image[48:, :] = split.astype(f32).astype(bf16)
    image[:48, :] = fold(unit_rows(pic[...])[0].astype(bf16))
    for source, target in ((tokens, own), (other_tokens, other)):
        turned[...] = source[...].T
        for chip in range(16):
            here = pl.ds(pl.multiple_of(chip * 96 + c * 48, 16), 48)
            target[chip * 48 : chip * 48 + 48, :] = turned[here, :]
    for k, out in enumerate((a0, a1, a2, a3)):
        at = pl.ds(pl.multiple_of(((y - k) & 3) * 384, 384), 384)
        acc = jnp.dot(own[...], adj[:, at], preferred_element_type=f32)
        acc = acc + jnp.dot(other[...], other_adj[:, at], preferred_element_type=f32)
        acc = acc.astype(bf16)
        out[:CUT, :] = acc[:CUT]
        out[CUT : 2 * CUT, :] = acc[384 : 384 + CUT]
        b_own[:, at] = jnp.where(low, acc[CUT:384], acc[384 + CUT :])
        b_out[:, at] = jnp.where(low, acc[384 + CUT :], acc[CUT:384])
        if k:
            out[2 * CUT :, :] = image[...]


def first_sum_kernel(
    place, a0, a1, a2, a3, b_own, b_in, image, a_own, near, column, *rest
):
    b0, b1, b2, b3, total = rest
    y, xh = place[0], place[2]
    total[...] = a0[...].astype(f32)
    for part in (a1, a2, a3):
        total[...] += part[: 2 * CUT, :].astype(f32)
    a_own[...] = total[pl.ds(pl.multiple_of(xh * CUT, 16), CUT), :]
    near[:CUT, :] = total[pl.ds(pl.multiple_of((1 - xh) * CUT, 16), CUT), :].astype(bf16)
    for k, out in enumerate((b0, b1, b2, b3)):
        at = pl.ds(pl.multiple_of(((y - k) & 3) * 384, 384), 384)
        both = b_own[:, at].astype(f32) + b_in[:, at].astype(f32)
        out[...] = both.astype(out.dtype)
    for target, first in ((near, CUT), (column, 0)):
        target[first : first + 64, :] = image[...]
        for k, part in enumerate((a1, a2, a3)):
            at = first + 64 + 64 * k
            target[at : at + 64, :] = part[2 * CUT :, :]


def tile_kernel(place, sharp, bias, i0, i1, i2, i3, other_text, along_z, a_own, *rest):
    b0, b1, b2, b3, rows, weight, g0, g1, g2, g3, t_own, t_out, images, texts, ids = rest
    for k in range(8):
        rows[k] = along_z[k, 48:, :]
    weight[:CUT, :] = (a_own[...] + i1[:CUT, :].astype(f32)).astype(bf16)
    total = b0[...]
    for part in (b1, b2, b3):
        total = total + part[...].astype(f32)
    weight[CUT:, :] = total.astype(bf16)
    y, xl, xh, c = place[0], place[1], place[2], place[3]
    for k, part in enumerate((i0, i1, i2, i3)):
        first = part.shape[0] - 256
        for j in range(4):
            at = k * 64 + j * 16
            here = first + j * 64
            images[at : at + 16, :] = unfold(part[here : here + 48, :])
            split = part[here + 48 : here + 64, :128].astype(f32)
            ids[at : at + 16, :] = (split[:, 0:1] * 64.0 + split[:, 1:2]).astype(jnp.int32)
    for k in range(8):
        texts[k * 16 : k * 16 + 16, :] = unfold(along_z[k, :48, :])
        texts[128 + k * 16 : 144 + k * 16, :] = unfold(other_text[k, :, :])
    sharpness, offset = sharp[0], bias[0]
    col = lax.broadcasted_iota(jnp.int32, (256, 256), 1)
    core = jnp.where(col < 128, c, 1 - c)
    first = ((xl * 4 + y) * 2 + xh) * 256
    index = first + (((col & 127) >> 4) * 2 + core) * 16 + (col & 15)
    dots = lax.dot_general(images[...], texts[...], BACK, preferred_element_type=f32)
    labels = (ids[...] == index).astype(f32)
    weights = sharpness * (jax.nn.sigmoid(sharpness * dots + offset) - labels)
    half = weights.astype(bf16)
    for k in range(4):
        part = jnp.dot(half[k * 64 : k * 64 + 64], texts[...], preferred_element_type=f32)
        for j, out in enumerate((g0, g1, g2, g3)):
            out[k * 48 : k * 48 + 48, :] = fold(part[j * 16 : j * 16 + 16]).astype(out.dtype)
    half = weights.T.astype(bf16)
    t_own[...] = jnp.dot(half[:128], images[...], preferred_element_type=f32)
    t_out[...] = jnp.dot(half[128:], images[...], preferred_element_type=f32).astype(bf16)


def send_back_kernel(place, t_own, t_in, weight, out):
    total = (t_own[...] + t_in[...].astype(f32)).astype(bf16)
    for k in range(8):
        out[k, :48, :] = fold(total[k * 16 : k * 16 + 16])
        out[k, 48:, :] = weight[k * 48 : k * 48 + 48, :]


def middle_kernel(place, back, cap, g0, g1, g2, g3, grad, pieces, h0, h1, h2, h3):
    total = back[0].astype(f32)
    for k in range(1, 8):
        total = total + back[k].astype(f32)
    grad[...] = back_through_norm(cap[...], unfold(total[:48]))
    piece = total[48:] * (1.0 / math.sqrt(98304))
    for k in range(8):
        pieces[k] = piece
    total = g0[...]
    for part in (g1, g2, g3):
        total = total + part[...].astype(f32)
    for k, out in enumerate((h0, h1, h2, h3)):
        out[...] = total[k * 48 : k * 48 + 48].astype(out.dtype)


def end_kernel(place, h0, h1, h2, h3, pic, pieces, image_grad, weight_grad):
    total = h0[...]
    for part in (h1, h2, h3):
        total = total + part[...].astype(f32)
    image_grad[...] = back_through_norm(pic[...], unfold(total))
    for k in range(4):
        weight_grad[:, k * 384 : k * 384 + 384] = pieces[k] + pieces[4 + k]


def project_kernel(place, adj, w, w_pair, other, other_pair, *rest):
    out, rows = rest[-2:]
    xl, c = place[1], place[3]
    for core, side, part in ((c, xl, w), (c, 1 - xl, w_pair), (1 - c, xl, other), (1 - c, 1 - xl, other_pair)):
        for k in range(2):
            at = pl.ds(pl.multiple_of(side * 768 + k * 384, 384), 384)
            for z in range(8):
                rows[z * 2 + core, :, at] = part[z, k * 48 : k * 48 + 48, :]
    for k in range(2):
        part = rows[k * 8 : k * 8 + 8].reshape(384, 1536)
        out[:, k * 384 : k * 384 + 384] = lax.dot_general(
            adj[...], part, BACK, preferred_element_type=f32
        ).astype(bf16)


def project(place, half, adj, parts, before=None):
    whole = pl.BlockSpec(memory_space=pltpu.VMEM)
    operands = [adj, *parts] + ([] if before is None else [before])
    in_specs = [whole] * 5 + ([] if before is None else [pl.BlockSpec(memory_space=pl.ANY)])
    return pl.pallas_call(
        project_kernel,
        grid_spec=pltpu.PrefetchScalarGridSpec(
            num_scalar_prefetch=1,
            grid=(1,),
            in_specs=in_specs,
            out_specs=pl.BlockSpec((384, 768), lambda i, place: (0, place[half])),
            scratch_shapes=[pltpu.VMEM((16, 48, 1536), bf16)],
        ),
        out_shape=shape(384, 1536),
        input_output_aliases={} if before is None else {6: 0},
        compiler_params=pltpu.CompilerParams(vmem_limit_bytes=16 * 2**20),
        cost_estimate=pl.CostEstimate(
            flops=2 * 384 * 768 * 1536, bytes_accessed=6 * 2**20, transcendentals=0
        ),
    )(place, *operands)


def per_device(
    picture_vectors_prenorm,
    caption_vectors_prenorm,
    matched_caption_ids,
    sharpness_coefficient,
    additive_offset_term,
    heads_mixed_concluding,
    dense_result_adjoint,
    dense_mapping_matrix,
):
    y, xl, xh, c = (lax.axis_index(name) for name in ("y", "xl", "xh", "c"))
    place = jnp.stack([y, xl, xh, c, 1 - xh]).astype(jnp.int32)
    other_adjoint = swap_cores(dense_result_adjoint)
    other_tokens = swap_cores(heads_mixed_concluding)

    (along_z,) = call(
        text_kernel, (shape(8, 144, 384),), place, caption_vectors_prenorm, dense_mapping_matrix
    )
    along_z = exchange(after(along_z, other_tokens, other_adjoint), "z")

    *a, b_own, b_out, image = call(
        weight_kernel,
        (
            shape(2 * CUT, 384),
            *[shape(2 * CUT + 64, 384)] * 3,
            shape(384 - CUT, 1536),
            shape(384 - CUT, 1536),
            shape(64, 384),
        ),
        place,
        matched_caption_ids,
        picture_vectors_prenorm,
        heads_mixed_concluding,
        other_tokens,
        dense_result_adjoint,
        other_adjoint,
        scratch=[
            pltpu.VMEM((1536, 384), bf16),
            pltpu.VMEM((768, 384), bf16),
            pltpu.VMEM((768, 384), bf16),
        ],
        spaces=(pltpu.SMEM,),
        flops=4 * 768 * 384 * 1536,
    )
    b_in = swap_halves(b_out)
    a_in = [turn(a[k], COLUMN, -k) for k in (1, 2, 3)]
    a_own, near, column, *b = call(
        first_sum_kernel,
        (
            shape(CUT, 384, dtype=f32),
            shape(CUT + 256, 384),
            shape(256, 384),
            shape(384 - CUT, 384, dtype=f32),
            *[shape(384 - CUT, 384)] * 3,
        ),
        place,
        a[0],
        *a_in,
        b_own,
        b_in,
        image,
        scratch=[pltpu.VMEM((2 * CUT, 384), f32)],
    )
    near_in = swap_halves(near)
    b = [b[0]] + [turn(b[k], COLUMN, -k) for k in (1, 2, 3)]
    pair_in, far_in = swap_pairs(column), swap_far(column)
    along_z = after(along_z, near)
    other_text = swap_cores(along_z[:, :48])
    here, weight_plane, *g, t_own, t_out = call(
        tile_kernel,
        (
            shape(8, 96, 384),
            shape(384, 384),
            shape(192, 384, dtype=f32),
            *[shape(192, 384)] * 3,
            shape(128, 1152, dtype=f32),
            shape(128, 1152),
        ),
        place,
        sharpness_coefficient,
        additive_offset_term,
        column,
        near_in,
        pair_in,
        far_in,
        other_text,
        along_z,
        a_own,
        *b,
        scratch=[
            pltpu.VMEM((256, 1152), bf16),
            pltpu.VMEM((256, 1152), bf16),
            pltpu.VMEM((256, 1), jnp.int32),
        ],
        spaces=(pltpu.SMEM, pltpu.SMEM),
        flops=6 * 256 * 256 * 1152,
    )

    pair = swap_pairs(here)
    there = swap_halves(here)
    there_pair = swap_pairs(there)

    t_in = swap_cores(t_out)
    (back,) = call(send_back_kernel, (shape(8, 96, 384),), place, t_own, t_in, weight_plane)
    other, other_pair = swap_cores(here), swap_cores(pair)
    back = exchange(back, "z")
    attn_grad = project(
        place, 2, dense_result_adjoint, (here, pair, other, other_pair)
    )

    g = [g[0]] + [turn(g[k], COLUMN, k) for k in (1, 2, 3)]
    text_grad, pieces, *h = call(
        middle_kernel,
        (
            shape(16, 1152, dtype=f32),
            shape(8, 48, 384, dtype=f32),
            shape(48, 384, dtype=f32),
            *[shape(48, 384)] * 3,
        ),
        place,
        after(back, attn_grad),
        caption_vectors_prenorm,
        *g,
    )
    pieces = exchange(pieces, ("xl", "y"))
    h = [h[0], swap_halves(h[1]), swap_pairs(h[2]), swap_far(h[3])]
    attn_grad = project(
        place,
        4,
        dense_result_adjoint,
        (there_pair, there, swap_cores(after(there_pair, h[0])), swap_cores(after(there, h[0]))),
        attn_grad,
    )
    image_grad, weight_grad = call(
        end_kernel,
        (shape(16, 1152, dtype=f32), shape(48, 1536, dtype=f32)),
        place,
        *h,
        picture_vectors_prenorm,
        after(pieces, attn_grad),
    )
    return (image_grad, text_grad, attn_grad, weight_grad)


def solution(mesh):
    chips = Mesh(mesh.devices.reshape(SIZES), AXES)
    everywhere = P(AXES, None)
    by_group = P(("xh", "z", "c"), None)
    return jax.shard_map(
        per_device,
        mesh=chips,
        in_specs=(
            everywhere,
            everywhere,
            P(AXES),
            P(),
            P(),
            everywhere,
            everywhere,
            by_group,
        ),
        out_specs=(everywhere, everywhere, everywhere, by_group),
        check_vma=False,
    )
```

```python
import math

import jax
import jax.numpy as jnp
from jax import lax
from jax.experimental import pallas as pl
from jax.experimental.pallas import tpu as pltpu
from jax.sharding import Mesh, PartitionSpec as P

stability_floor = 1e-06
f32, bf16 = jnp.float32, jnp.bfloat16

AXES = ("xl", "y", "xh", "z", "c")
SIZES = (2, 4, 2, 8, 2)
ROW = (("xl", "xh"), (0, 2, 1, 3))
COLUMN = ("y", (0, 1, 2, 3))
CUT = 192
BACK = (((1,), (1,)), ((), ()))


def swap_cores(x):
    return lax.ppermute(x, "c", [(0, 1), (1, 0)])


def turn(x, ring, by):
    axes, at = ring
    return lax.ppermute(x, axes, [(at[i], at[(i + by) % 4]) for i in range(4)])


def swap_halves(x):
    axes, at = ROW
    return lax.ppermute(x, axes, [(at[i], at[3 - i]) for i in range(4)])


def swap_pairs(x):
    return lax.ppermute(x, "xl", [(0, 1), (1, 0)])


def swap_far(x):
    return lax.ppermute(x, "xh", [(0, 1), (1, 0)])


def exchange(x, axes):
    return lax.all_to_all(x, axes, 0, 0, tiled=True)


def after(x, *earlier):
    return lax.optimization_barrier((x, *earlier))[0]


def fold(x):
    return jnp.concatenate([x[:, i * 384 : (i + 1) * 384] for i in range(3)], axis=0)


def unfold(x):
    return jnp.concatenate([x[i * 16 : (i + 1) * 16] for i in range(3)], axis=1)


def unit_rows(raw):
    row_scale = lax.rsqrt(jnp.sum(raw * raw, axis=1, keepdims=True) + stability_floor)
    return raw * row_scale, row_scale


def back_through_norm(raw, row_grad):
    normed, row_scale = unit_rows(raw)
    along_unit = jnp.sum(normed * row_grad, axis=1, keepdims=True)
    return (row_grad - normed * along_unit) * row_scale


def call(kernel, outs, place, *operands, scratch=(), flops=0, spaces=()):
    moved = sum(math.prod(o.shape) * o.dtype.itemsize for o in (*outs, *operands))
    spaces = tuple(spaces) + (pltpu.VMEM,) * (len(operands) - len(spaces))
    return pl.pallas_call(
        kernel,
        out_shape=tuple(outs),
        in_specs=[pl.BlockSpec(memory_space=space) for space in (pltpu.SMEM, *spaces)],
        out_specs=tuple(pl.BlockSpec(memory_space=pltpu.VMEM) for _ in outs),
        scratch_shapes=scratch,
        compiler_params=pltpu.CompilerParams(vmem_limit_bytes=16 * 2**20),
        cost_estimate=pl.CostEstimate(flops=flops, bytes_accessed=moved, transcendentals=0),
    )(place, *operands)


def shape(*dims, dtype=bf16):
    return jax.ShapeDtypeStruct(dims, dtype)


def text_kernel(place, cap, rows, z_out):
    text = fold(unit_rows(cap[...])[0].astype(bf16))
    piece = rows[:, pl.ds(pl.multiple_of(place[1] * 768, 384), 768)]
    for k in range(8):
        z_out[k, :48, :] = text
        z_out[k, 48:96, :] = piece[:, :384]
        z_out[k, 96:, :] = piece[:, 384:]


def weight_kernel(place, ids, pic, tokens, other_tokens, adj, other_adj, *rest):
    a0, a1, a2, a3, b_own, b_out, image, turned, both, block = rest
    y, low, c = place[0], place[2] == 0, place[3]
    line = lax.broadcasted_iota(jnp.int32, (16, 384), 0)
    number = jnp.zeros((16, 384), jnp.int32)
    for i in range(16):
        number = jnp.where(line == i, ids[i], number)
    lane = lax.broadcasted_iota(jnp.int32, (16, 384), 1)
    split = jnp.where(lane == 0, number >> 6, jnp.where(lane == 1, number & 63, 0))
    image[48:, :] = split.astype(f32).astype(bf16)
    image[:48, :] = fold(unit_rows(pic[...])[0].astype(bf16))
    for source, first in ((tokens, 0), (other_tokens, 384)):
        turned[...] = source[...].T
        for chip in range(16):
            here = pl.ds(pl.multiple_of(chip * 96 + c * 48, 16), 48)
            both[chip * 48 : chip * 48 + 48, first : first + 384] = turned[here, :]
    for k, out in enumerate((a0, a1, a2, a3)):
        at = pl.ds(pl.multiple_of(((y - k) & 3) * 384, 384), 384)
        block[:384, :] = adj[:, at]
        block[384:, :] = other_adj[:, at]
        acc = jnp.dot(both[...], block[...], preferred_element_type=f32).astype(bf16)
        out[:CUT, :] = acc[:CUT]
        out[CUT : 2 * CUT, :] = acc[384 : 384 + CUT]
        b_own[:, at] = jnp.where(low, acc[CUT:384], acc[384 + CUT :])
        b_out[:, at] = jnp.where(low, acc[384 + CUT :], acc[CUT:384])
        if k:
            out[2 * CUT :, :] = image[...]


def first_sum_kernel(
    place, a0, a1, a2, a3, b_own, b_in, image, a_own, near, column, *rest
):
    b0, b1, b2, b3, total = rest
    y, xh = place[0], place[2]
    del total
    for first, out in ((xh, a_own), (1 - xh, near)):
        here = pl.ds(pl.multiple_of(first * CUT, 16), CUT)
        half = a0[here, :].astype(f32)
        for part in (a1, a2, a3):
            half = half + part[here, :].astype(f32)
        out[:CUT, :] = half.astype(out.dtype)
    for k, out in enumerate((b0, b1, b2, b3)):
        at = pl.ds(pl.multiple_of(((y - k) & 3) * 384, 384), 384)
        both = b_own[:, at].astype(f32) + b_in[:, at].astype(f32)
        out[...] = both.astype(out.dtype)
    for target, first in ((near, CUT), (column, 0)):
        target[first : first + 64, :] = image[...]
        for k, part in enumerate((a1, a2, a3)):
            at = first + 64 + 64 * k
            target[at : at + 64, :] = part[2 * CUT :, :]


def tile_kernel(place, sharp, bias, i0, i1, i2, i3, other_text, along_z, a_own, *rest):
    b0, b1, b2, b3, rows, weight, g0, g1, g2, g3, t_own, t_out, images, texts, ids = rest
    for k in range(8):
        rows[k] = along_z[k, 48:, :]
    weight[:CUT, :] = (a_own[...] + i1[:CUT, :].astype(f32)).astype(bf16)
    total = b0[...]
    for part in (b1, b2, b3):
        total = total + part[...].astype(f32)
    weight[CUT:, :] = total.astype(bf16)
    y, xl, xh, c = place[0], place[1], place[2], place[3]
    for k, part in enumerate((i0, i1, i2, i3)):
        first = part.shape[0] - 256
        for j in range(4):
            at = k * 64 + j * 16
            here = first + j * 64
            images[at : at + 16, :] = unfold(part[here : here + 48, :])
            split = part[here + 48 : here + 64, :128].astype(f32)
            ids[at : at + 16, :] = (split[:, 0:1] * 64.0 + split[:, 1:2]).astype(jnp.int32)
    for k in range(8):
        texts[k * 16 : k * 16 + 16, :] = unfold(along_z[k, :48, :])
        texts[128 + k * 16 : 144 + k * 16, :] = unfold(other_text[k, :, :])
    sharpness, offset = sharp[0], bias[0]
    col = lax.broadcasted_iota(jnp.int32, (256, 256), 1)
    core = jnp.where(col < 128, c, 1 - c)
    first = ((xl * 4 + y) * 2 + xh) * 256
    index = first + (((col & 127) >> 4) * 2 + core) * 16 + (col & 15)
    dots = lax.dot_general(images[...], texts[...], BACK, preferred_element_type=f32)
    labels = (ids[...] == index).astype(f32)
    weights = sharpness * (jax.nn.sigmoid(sharpness * dots + offset) - labels)
    half = weights.astype(bf16)
    for k in range(4):
        part = jnp.dot(half[k * 64 : k * 64 + 64], texts[...], preferred_element_type=f32)
        for j, out in enumerate((g0, g1, g2, g3)):
            out[k * 48 : k * 48 + 48, :] = fold(part[j * 16 : j * 16 + 16]).astype(out.dtype)
    half = weights.T.astype(bf16)
    t_own[...] = jnp.dot(half[:128], images[...], preferred_element_type=f32)
    t_out[...] = jnp.dot(half[128:], images[...], preferred_element_type=f32).astype(bf16)


def send_back_kernel(place, t_own, t_in, weight, out):
    total = (t_own[...] + t_in[...].astype(f32)).astype(bf16)
    for k in range(8):
        out[k, :48, :] = fold(total[k * 16 : k * 16 + 16])
        out[k, 48:, :] = weight[k * 48 : k * 48 + 48, :]


def middle_kernel(place, back, cap, g0, g1, g2, g3, grad, pieces, h0, h1, h2, h3):
    total = back[0].astype(f32)
    for k in range(1, 8):
        total = total + back[k].astype(f32)
    grad[...] = back_through_norm(cap[...], unfold(total[:48]))
    piece = total[48:].astype(bf16)
    for k in range(8):
        pieces[k] = piece
    total = g0[...]
    for part in (g1, g2, g3):
        total = total + part[...].astype(f32)
    for k, out in enumerate((h0, h1, h2, h3)):
        out[...] = total[k * 48 : k * 48 + 48].astype(out.dtype)


def end_kernel(place, h0, h1, h2, h3, pic, pieces, image_grad, weight_grad):
    total = h0[...]
    for part in (h1, h2, h3):
        total = total + part[...].astype(f32)
    image_grad[...] = back_through_norm(pic[...], unfold(total))
    for k in range(4):
        piece = pieces[k].astype(f32) + pieces[4 + k].astype(f32)
        weight_grad[:, k * 384 : k * 384 + 384] = piece * (1.0 / math.sqrt(98304))


def project_kernel(place, adj, w, w_pair, other, other_pair, *rest):
    out, rows = rest[-2:]
    xl, c = place[1], place[3]
    for core, side, part in ((c, xl, w), (c, 1 - xl, w_pair), (1 - c, xl, other), (1 - c, 1 - xl, other_pair)):
        for k in range(2):
            at = pl.ds(pl.multiple_of(side * 768 + k * 384, 384), 384)
            for z in range(8):
                rows[z * 2 + core, :, at] = part[z, k * 48 : k * 48 + 48, :]
    for k in range(2):
        part = rows[k * 8 : k * 8 + 8].reshape(384, 1536)
        out[:, k * 384 : k * 384 + 384] = lax.dot_general(
            adj[...], part, BACK, preferred_element_type=f32
        ).astype(bf16)


def project(place, half, adj, parts, before=None):
    whole = pl.BlockSpec(memory_space=pltpu.VMEM)
    operands = [adj, *parts] + ([] if before is None else [before])
    in_specs = [whole] * 5 + ([] if before is None else [pl.BlockSpec(memory_space=pl.ANY)])
    return pl.pallas_call(
        project_kernel,
        grid_spec=pltpu.PrefetchScalarGridSpec(
            num_scalar_prefetch=1,
            grid=(1,),
            in_specs=in_specs,
            out_specs=pl.BlockSpec((384, 768), lambda i, place: (0, place[half])),
            scratch_shapes=[pltpu.VMEM((16, 48, 1536), bf16)],
        ),
        out_shape=shape(384, 1536),
        input_output_aliases={} if before is None else {6: 0},
        compiler_params=pltpu.CompilerParams(vmem_limit_bytes=16 * 2**20),
        cost_estimate=pl.CostEstimate(
            flops=2 * 384 * 768 * 1536, bytes_accessed=6 * 2**20, transcendentals=0
        ),
    )(place, *operands)


def per_device(
    picture_vectors_prenorm,
    caption_vectors_prenorm,
    matched_caption_ids,
    sharpness_coefficient,
    additive_offset_term,
    heads_mixed_concluding,
    dense_result_adjoint,
    dense_mapping_matrix,
):
    y, xl, xh, c = (lax.axis_index(name) for name in ("y", "xl", "xh", "c"))
    place = jnp.stack([y, xl, xh, c, 1 - xh]).astype(jnp.int32)
    other_adjoint = swap_cores(dense_result_adjoint)
    other_tokens = swap_cores(heads_mixed_concluding)

    (along_z,) = call(
        text_kernel, (shape(8, 144, 384),), place, caption_vectors_prenorm, dense_mapping_matrix
    )
    along_z = exchange(after(along_z, other_tokens), "z")

    *a, b_own, b_out, image = call(
        weight_kernel,
        (
            shape(2 * CUT, 384),
            *[shape(2 * CUT + 64, 384)] * 3,
            shape(384 - CUT, 1536),
            shape(384 - CUT, 1536),
            shape(64, 384),
        ),
        place,
        matched_caption_ids,
        picture_vectors_prenorm,
        heads_mixed_concluding,
        other_tokens,
        dense_result_adjoint,
        other_adjoint,
        scratch=[
            pltpu.VMEM((1536, 384), bf16),
            pltpu.VMEM((768, 768), bf16),
            pltpu.VMEM((768, 384), bf16),
        ],
        spaces=(pltpu.SMEM,),
        flops=4 * 768 * 384 * 1536,
    )
    b_in = swap_halves(b_out)
    a_in = [turn(a[k], COLUMN, -k) for k in (1, 2, 3)]
    a_own, near, column, *b = call(
        first_sum_kernel,
        (
            shape(CUT, 384, dtype=f32),
            shape(CUT + 256, 384),
            shape(256, 384),
            shape(384 - CUT, 384, dtype=f32),
            *[shape(384 - CUT, 384)] * 3,
        ),
        place,
        a[0],
        *a_in,
        b_own,
        b_in,
        image,
        scratch=[pltpu.VMEM((2 * CUT, 384), f32)],
    )
    near_in = swap_halves(near)
    b = [b[0]] + [turn(b[k], COLUMN, -k) for k in (1, 2, 3)]
    pair_in, far_in = swap_pairs(column), swap_far(column)
    along_z = after(along_z, near)
    other_text = swap_cores(along_z[:, :48])
    here, weight_plane, *g, t_own, t_out = call(
        tile_kernel,
        (
            shape(8, 96, 384),
            shape(384, 384),
            shape(192, 384, dtype=f32),
            *[shape(192, 384)] * 3,
            shape(128, 1152, dtype=f32),
            shape(128, 1152),
        ),
        place,
        sharpness_coefficient,
        additive_offset_term,
        column,
        near_in,
        pair_in,
        far_in,
        other_text,
        along_z,
        a_own,
        *b,
        scratch=[
            pltpu.VMEM((256, 1152), bf16),
            pltpu.VMEM((256, 1152), bf16),
            pltpu.VMEM((256, 1), jnp.int32),
        ],
        spaces=(pltpu.SMEM, pltpu.SMEM),
        flops=6 * 256 * 256 * 1152,
    )

    pair = swap_pairs(here)
    there = swap_halves(here)
    there_pair = swap_pairs(there)

    t_in = swap_cores(t_out)
    (back,) = call(send_back_kernel, (shape(8, 96, 384),), place, t_own, t_in, weight_plane)
    other, other_pair = swap_cores(here), swap_cores(pair)
    back = exchange(back, "z")
    attn_grad = project(
        place, 2, dense_result_adjoint, (here, pair, other, other_pair)
    )

    g = [g[0]] + [turn(g[k], COLUMN, k) for k in (1, 2, 3)]
    text_grad, pieces, *h = call(
        middle_kernel,
        (
            shape(16, 1152, dtype=f32),
            shape(8, 48, 384),
            shape(48, 384, dtype=f32),
            *[shape(48, 384)] * 3,
        ),
        place,
        after(back, attn_grad),
        caption_vectors_prenorm,
        *g,
    )
    pieces = exchange(pieces, ("xl", "y"))
    h = [h[0], swap_halves(h[1]), swap_pairs(h[2]), swap_far(h[3])]
    attn_grad = project(
        place,
        4,
        dense_result_adjoint,
        (there_pair, there, swap_cores(after(there_pair, h[0])), swap_cores(after(there, h[0]))),
        attn_grad,
    )
    image_grad, weight_grad = call(
        end_kernel,
        (shape(16, 1152, dtype=f32), shape(48, 1536, dtype=f32)),
        place,
        *h,
        picture_vectors_prenorm,
        after(pieces, attn_grad),
    )
    return (image_grad, text_grad, attn_grad, weight_grad)


def solution(mesh):
    chips = Mesh(mesh.devices.reshape(SIZES), AXES)
    everywhere = P(AXES, None)
    by_group = P(("xh", "z", "c"), None)
    return jax.shard_map(
        per_device,
        mesh=chips,
        in_specs=(
            everywhere,
            everywhere,
            P(AXES),
            P(),
            P(),
            everywhere,
            everywhere,
            by_group,
        ),
        out_specs=(everywhere, everywhere, everywhere, by_group),
        check_vma=False,
    )
```

```python
import math

import jax
import jax.numpy as jnp
from jax import lax
from jax.experimental import pallas as pl
from jax.experimental.pallas import tpu as pltpu
from jax.sharding import Mesh, PartitionSpec as P

stability_floor = 1e-06
f32, bf16 = jnp.float32, jnp.bfloat16

AXES = ("xl", "y", "xh", "z", "c")
SIZES = (2, 4, 2, 8, 2)
ROW = (("xl", "xh"), (0, 2, 1, 3))
COLUMN = ("y", (0, 1, 2, 3))
CUT = 192
BACK = (((1,), (1,)), ((), ()))


def swap_cores(x):
    return lax.ppermute(x, "c", [(0, 1), (1, 0)])


def turn(x, ring, by):
    axes, at = ring
    return lax.ppermute(x, axes, [(at[i], at[(i + by) % 4]) for i in range(4)])


def swap_halves(x):
    axes, at = ROW
    return lax.ppermute(x, axes, [(at[i], at[3 - i]) for i in range(4)])


def swap_pairs(x):
    return lax.ppermute(x, "xl", [(0, 1), (1, 0)])


def swap_far(x):
    return lax.ppermute(x, "xh", [(0, 1), (1, 0)])


def exchange(x, axes):
    return lax.all_to_all(x, axes, 0, 0, tiled=True)


def after(x, *earlier):
    return lax.optimization_barrier((x, *earlier))[0]


def fold(x):
    return jnp.concatenate([x[:, i * 384 : (i + 1) * 384] for i in range(3)], axis=0)


def unfold(x):
    return jnp.concatenate([x[i * 16 : (i + 1) * 16] for i in range(3)], axis=1)


def unit_rows(raw):
    row_scale = lax.rsqrt(jnp.sum(raw * raw, axis=1, keepdims=True) + stability_floor)
    return raw * row_scale, row_scale


def back_through_norm(raw, row_grad):
    normed, row_scale = unit_rows(raw)
    along_unit = jnp.sum(normed * row_grad, axis=1, keepdims=True)
    return (row_grad - normed * along_unit) * row_scale


def call(kernel, outs, place, *operands, scratch=(), flops=0, spaces=()):
    moved = sum(math.prod(o.shape) * o.dtype.itemsize for o in (*outs, *operands))
    spaces = tuple(spaces) + (pltpu.VMEM,) * (len(operands) - len(spaces))
    return pl.pallas_call(
        kernel,
        out_shape=tuple(outs),
        in_specs=[pl.BlockSpec(memory_space=space) for space in (pltpu.SMEM, *spaces)],
        out_specs=tuple(pl.BlockSpec(memory_space=pltpu.VMEM) for _ in outs),
        scratch_shapes=scratch,
        compiler_params=pltpu.CompilerParams(vmem_limit_bytes=16 * 2**20),
        cost_estimate=pl.CostEstimate(flops=flops, bytes_accessed=moved, transcendentals=0),
    )(place, *operands)


def shape(*dims, dtype=bf16):
    return jax.ShapeDtypeStruct(dims, dtype)


def text_kernel(place, cap, rows, z_out):
    text = fold(unit_rows(cap[...])[0].astype(bf16))
    piece = rows[:, pl.ds(pl.multiple_of(place[1] * 768, 384), 768)]
    for k in range(8):
        z_out[k, :48, :] = text
        z_out[k, 48:96, :] = piece[:, :384]
        z_out[k, 96:, :] = piece[:, 384:]


def weight_kernel(place, ids, pic, tokens, other_tokens, adj, other_adj, *rest):
    a0, a1, a2, a3, b_own, b_out, image, turned, both, block = rest
    y, low, c = place[0], place[2] == 0, place[3]
    line = lax.broadcasted_iota(jnp.int32, (16, 384), 0)
    number = jnp.zeros((16, 384), jnp.int32)
    for i in range(16):
        number = jnp.where(line == i, ids[i], number)
    lane = lax.broadcasted_iota(jnp.int32, (16, 384), 1)
    split = jnp.where(lane == 0, number >> 6, jnp.where(lane == 1, number & 63, 0))
    image[48:, :] = split.astype(f32).astype(bf16)
    image[:48, :] = fold(unit_rows(pic[...])[0].astype(bf16))
    for source, first in ((tokens, 0), (other_tokens, 384)):
        turned[...] = source[...].T
        for chip in range(16):
            here = pl.ds(pl.multiple_of(chip * 96 + c * 48, 16), 48)
            both[chip * 48 : chip * 48 + 48, first : first + 384] = turned[here, :]
    for k, out in enumerate((a0, a1, a2, a3)):
        at = pl.ds(pl.multiple_of(((y - k) & 3) * 384, 384), 384)
        block[:384, :] = adj[:, at]
        block[384:, :] = other_adj[:, at]
        acc = jnp.dot(both[...], block[...], preferred_element_type=f32).astype(bf16)
        out[:CUT, :] = acc[:CUT]
        out[CUT : 2 * CUT, :] = acc[384 : 384 + CUT]
        b_own[:, at] = jnp.where(low, acc[CUT:384], acc[384 + CUT :])
        b_out[:, at] = jnp.where(low, acc[384 + CUT :], acc[CUT:384])
        if k:
            out[2 * CUT :, :] = image[...]


def first_sum_kernel(
    place, a0, a1, a2, a3, b_own, b_in, image, a_own, near, column, *rest
):
    b0, b1, b2, b3, total = rest
    y, xh = place[0], place[2]
    del total
    for first, out in ((xh, a_own), (1 - xh, near)):
        here = pl.ds(pl.multiple_of(first * CUT, 16), CUT)
        half = a0[here, :].astype(f32)
        for part in (a1, a2, a3):
            half = half + part[here, :].astype(f32)
        out[:CUT, :] = half.astype(out.dtype)
    for k, out in enumerate((b0, b1, b2, b3)):
        at = pl.ds(pl.multiple_of(((y - k) & 3) * 384, 384), 384)
        both = b_own[:, at].astype(f32) + b_in[:, at].astype(f32)
        out[...] = both.astype(out.dtype)
    for target, first in ((near, CUT), (column, 0)):
        target[first : first + 64, :] = image[...]
        for k, part in enumerate((a1, a2, a3)):
            at = first + 64 + 64 * k
            target[at : at + 64, :] = part[2 * CUT :, :]


def tile_kernel(place, sharp, bias, i0, i1, i2, i3, other_text, along_z, a_own, *rest):
    b0, b1, b2, b3, rows, weight, g0, g1, g2, g3, t_own, t_out, images, texts, ids = rest
    for k in range(8):
        rows[k] = along_z[k, 48:, :]
    weight[:CUT, :] = (a_own[...] + i1[:CUT, :].astype(f32)).astype(bf16)
    total = b0[...]
    for part in (b1, b2, b3):
        total = total + part[...].astype(f32)
    weight[CUT:, :] = total.astype(bf16)
    y, xl, xh, c = place[0], place[1], place[2], place[3]
    for k, part in enumerate((i0, i1, i2, i3)):
        first = part.shape[0] - 256
        for j in range(4):
            at = k * 64 + j * 16
            here = first + j * 64
            images[at : at + 16, :] = unfold(part[here : here + 48, :])
            split = part[here + 48 : here + 64, :128].astype(f32)
            ids[at : at + 16, :] = (split[:, 0:1] * 64.0 + split[:, 1:2]).astype(jnp.int32)
    for k in range(8):
        texts[k * 16 : k * 16 + 16, :] = unfold(along_z[k, :48, :])
        texts[128 + k * 16 : 144 + k * 16, :] = unfold(other_text[k, :, :])
    sharpness, offset = sharp[0], bias[0]
    col = lax.broadcasted_iota(jnp.int32, (256, 256), 1)
    core = jnp.where(col < 128, c, 1 - c)
    first = ((xl * 4 + y) * 2 + xh) * 256
    index = first + (((col & 127) >> 4) * 2 + core) * 16 + (col & 15)
    dots = lax.dot_general(images[...], texts[...], BACK, preferred_element_type=f32)
    labels = (ids[...] == index).astype(f32)
    weights = sharpness * (jax.nn.sigmoid(sharpness * dots + offset) - labels)
    half = weights.astype(bf16)
    for k in range(4):
        part = jnp.dot(half[k * 64 : k * 64 + 64], texts[...], preferred_element_type=f32)
        for j, out in enumerate((g0, g1, g2, g3)):
            out[k * 48 : k * 48 + 48, :] = fold(part[j * 16 : j * 16 + 16]).astype(out.dtype)
    half = weights.T.astype(bf16)
    t_own[...] = jnp.dot(half[:128], images[...], preferred_element_type=f32)
    t_out[...] = jnp.dot(half[128:], images[...], preferred_element_type=f32).astype(bf16)


def send_back_kernel(place, t_own, t_in, weight, out):
    total = (t_own[...] + t_in[...].astype(f32)).astype(bf16)
    for k in range(8):
        out[k, :48, :] = fold(total[k * 16 : k * 16 + 16])
        out[k, 48:, :] = weight[k * 48 : k * 48 + 48, :]


def middle_kernel(place, back, cap, g0, g1, g2, g3, grad, pieces, h0, h1, h2, h3):
    total = back[0].astype(f32)
    for k in range(1, 8):
        total = total + back[k].astype(f32)
    grad[...] = back_through_norm(cap[...], unfold(total[:48]))
    piece = total[48:].astype(bf16)
    for k in range(8):
        pieces[k] = piece
    total = g0[...]
    for part in (g1, g2, g3):
        total = total + part[...].astype(f32)
    for k, out in enumerate((h0, h1, h2, h3)):
        out[...] = total[k * 48 : k * 48 + 48].astype(out.dtype)


def end_kernel(place, h0, h1, h2, h3, pic, pieces, image_grad, weight_grad):
    total = h0[...]
    for part in (h1, h2, h3):
        total = total + part[...].astype(f32)
    image_grad[...] = back_through_norm(pic[...], unfold(total))
    for k in range(4):
        piece = pieces[k].astype(f32) + pieces[4 + k].astype(f32)
        weight_grad[:, k * 384 : k * 384 + 384] = piece * (1.0 / math.sqrt(98304))


def project_kernel(place, adj, w, w_pair, other, other_pair, *rest):
    out, rows = rest[-2:]
    xl, c = place[1], place[3]
    for core, side, part in ((c, xl, w), (c, 1 - xl, w_pair), (1 - c, xl, other), (1 - c, 1 - xl, other_pair)):
        for k in range(2):
            at = pl.ds(pl.multiple_of(side * 768 + k * 384, 384), 384)
            for z in range(8):
                rows[z * 2 + core, :, at] = part[z, k * 48 : k * 48 + 48, :]
    for k in range(2):
        part = rows[k * 8 : k * 8 + 8].reshape(384, 1536)
        out[:, k * 384 : k * 384 + 384] = lax.dot_general(
            adj[...], part, BACK, preferred_element_type=f32
        ).astype(bf16)


def project(place, half, adj, parts, before=None):
    whole = pl.BlockSpec(memory_space=pltpu.VMEM)
    operands = [adj, *parts] + ([] if before is None else [before])
    in_specs = [whole] * 5 + ([] if before is None else [pl.BlockSpec(memory_space=pl.ANY)])
    return pl.pallas_call(
        project_kernel,
        grid_spec=pltpu.PrefetchScalarGridSpec(
            num_scalar_prefetch=1,
            grid=(1,),
            in_specs=in_specs,
            out_specs=pl.BlockSpec((384, 768), lambda i, place: (0, place[half])),
            scratch_shapes=[pltpu.VMEM((16, 48, 1536), bf16)],
        ),
        out_shape=shape(384, 1536),
        input_output_aliases={} if before is None else {6: 0},
        compiler_params=pltpu.CompilerParams(vmem_limit_bytes=16 * 2**20),
        cost_estimate=pl.CostEstimate(
            flops=2 * 384 * 768 * 1536, bytes_accessed=6 * 2**20, transcendentals=0
        ),
    )(place, *operands)


def per_device(
    picture_vectors_prenorm,
    caption_vectors_prenorm,
    matched_caption_ids,
    sharpness_coefficient,
    additive_offset_term,
    heads_mixed_concluding,
    dense_result_adjoint,
    dense_mapping_matrix,
):
    y, xl, xh, c = (lax.axis_index(name) for name in ("y", "xl", "xh", "c"))
    place = jnp.stack([y, xl, xh, c, 1 - xh]).astype(jnp.int32)
    other_adjoint = swap_cores(dense_result_adjoint)
    other_tokens = swap_cores(heads_mixed_concluding)

    (along_z,) = call(
        text_kernel, (shape(8, 144, 384),), place, caption_vectors_prenorm, dense_mapping_matrix
    )
    along_z = exchange(after(along_z, other_tokens), "z")

    *a, b_own, b_out, image = call(
        weight_kernel,
        (
            shape(2 * CUT, 384),
            *[shape(2 * CUT + 64, 384)] * 3,
            shape(384 - CUT, 1536),
            shape(384 - CUT, 1536),
            shape(64, 384),
        ),
        place,
        matched_caption_ids,
        picture_vectors_prenorm,
        heads_mixed_concluding,
        other_tokens,
        dense_result_adjoint,
        other_adjoint,
        scratch=[
            pltpu.VMEM((1536, 384), bf16),
            pltpu.VMEM((768, 768), bf16),
            pltpu.VMEM((768, 384), bf16),
        ],
        spaces=(pltpu.SMEM,),
        flops=4 * 768 * 384 * 1536,
    )
    b_in = swap_halves(b_out)
    a_in = [turn(a[k], COLUMN, -k) for k in (1, 2, 3)]
    a_own, near, column, *b = call(
        first_sum_kernel,
        (
            shape(CUT, 384, dtype=f32),
            shape(CUT + 256, 384),
            shape(256, 384),
            shape(384 - CUT, 384, dtype=f32),
            *[shape(384 - CUT, 384)] * 3,
        ),
        place,
        a[0],
        *a_in,
        b_own,
        b_in,
        image,
        scratch=[pltpu.VMEM((2 * CUT, 384), f32)],
    )
    near_in = swap_halves(near)
    b = [b[0]] + [turn(b[k], COLUMN, -k) for k in (1, 2, 3)]
    along_z = after(along_z, near)
    other_text = swap_cores(along_z[:, :48])
    sent = after(column, other_text)
    pair_in, far_in = swap_pairs(sent), swap_far(sent)
    here, weight_plane, *g, t_own, t_out = call(
        tile_kernel,
        (
            shape(8, 96, 384),
            shape(384, 384),
            shape(192, 384, dtype=f32),
            *[shape(192, 384)] * 3,
            shape(128, 1152, dtype=f32),
            shape(128, 1152),
        ),
        place,
        sharpness_coefficient,
        additive_offset_term,
        column,
        near_in,
        pair_in,
        far_in,
        other_text,
        along_z,
        a_own,
        *b,
        scratch=[
            pltpu.VMEM((256, 1152), bf16),
            pltpu.VMEM((256, 1152), bf16),
            pltpu.VMEM((256, 1), jnp.int32),
        ],
        spaces=(pltpu.SMEM, pltpu.SMEM),
        flops=6 * 256 * 256 * 1152,
    )

    pair = swap_pairs(here)
    there = swap_halves(here)
    there_pair = swap_pairs(there)

    t_in = swap_cores(t_out)
    (back,) = call(send_back_kernel, (shape(8, 96, 384),), place, t_own, t_in, weight_plane)
    other, other_pair = swap_cores(here), swap_cores(pair)
    back = exchange(back, "z")
    attn_grad = project(
        place, 2, dense_result_adjoint, (here, pair, other, other_pair)
    )

    g = [g[0]] + [turn(g[k], COLUMN, k) for k in (1, 2, 3)]
    text_grad, pieces, *h = call(
        middle_kernel,
        (
            shape(16, 1152, dtype=f32),
            shape(8, 48, 384),
            shape(48, 384, dtype=f32),
            *[shape(48, 384)] * 3,
        ),
        place,
        after(back, attn_grad),
        caption_vectors_prenorm,
        *g,
    )
    pieces = exchange(pieces, ("xl", "y"))
    h = [h[0], swap_halves(h[1]), swap_pairs(h[2]), swap_far(h[3])]
    attn_grad = project(
        place,
        4,
        dense_result_adjoint,
        (there_pair, there, swap_cores(after(there_pair, h[0])), swap_cores(after(there, h[0]))),
        attn_grad,
    )
    image_grad, weight_grad = call(
        end_kernel,
        (shape(16, 1152, dtype=f32), shape(48, 1536, dtype=f32)),
        place,
        *h,
        picture_vectors_prenorm,
        after(pieces, attn_grad),
    )
    return (image_grad, text_grad, attn_grad, weight_grad)


def solution(mesh):
    chips = Mesh(mesh.devices.reshape(SIZES), AXES)
    everywhere = P(AXES, None)
    by_group = P(("xh", "z", "c"), None)
    return jax.shard_map(
        per_device,
        mesh=chips,
        in_specs=(
            everywhere,
            everywhere,
            P(AXES),
            P(),
            P(),
            everywhere,
            everywhere,
            by_group,
        ),
        out_specs=(everywhere, everywhere, everywhere, by_group),
        check_vma=False,
    )
```

```python
import math

import jax
import jax.numpy as jnp
from jax import lax
from jax.experimental import pallas as pl
from jax.experimental.pallas import tpu as pltpu
from jax.sharding import Mesh, PartitionSpec as P

stability_floor = 1e-06
f32, bf16 = jnp.float32, jnp.bfloat16

AXES = ("xl", "y", "xh", "z", "c")
SIZES = (2, 4, 2, 8, 2)
ROW = (("xl", "xh"), (0, 2, 1, 3))
COLUMN = ("y", (0, 1, 2, 3))
CUT = 192
BACK = (((1,), (1,)), ((), ()))


def swap_cores(x):
    return lax.ppermute(x, "c", [(0, 1), (1, 0)])


def turn(x, ring, by):
    axes, at = ring
    return lax.ppermute(x, axes, [(at[i], at[(i + by) % 4]) for i in range(4)])


def swap_halves(x):
    axes, at = ROW
    return lax.ppermute(x, axes, [(at[i], at[3 - i]) for i in range(4)])


def swap_pairs(x):
    return lax.ppermute(x, "xl", [(0, 1), (1, 0)])


def swap_far(x):
    return lax.ppermute(x, "xh", [(0, 1), (1, 0)])


def exchange(x, axes):
    return lax.all_to_all(x, axes, 0, 0, tiled=True)


def after(x, *earlier):
    return lax.optimization_barrier((x, *earlier))[0]


def fold(x):
    return jnp.concatenate([x[:, i * 384 : (i + 1) * 384] for i in range(3)], axis=0)


def unfold(x):
    return jnp.concatenate([x[i * 16 : (i + 1) * 16] for i in range(3)], axis=1)


def unit_rows(raw):
    row_scale = lax.rsqrt(jnp.sum(raw * raw, axis=1, keepdims=True) + stability_floor)
    return raw * row_scale, row_scale


def back_through_norm(raw, row_grad):
    normed, row_scale = unit_rows(raw)
    along_unit = jnp.sum(normed * row_grad, axis=1, keepdims=True)
    return (row_grad - normed * along_unit) * row_scale


def call(kernel, outs, place, *operands, scratch=(), flops=0, spaces=()):
    moved = sum(math.prod(o.shape) * o.dtype.itemsize for o in (*outs, *operands))
    spaces = tuple(spaces) + (pltpu.VMEM,) * (len(operands) - len(spaces))
    return pl.pallas_call(
        kernel,
        out_shape=tuple(outs),
        in_specs=[pl.BlockSpec(memory_space=space) for space in (pltpu.SMEM, *spaces)],
        out_specs=tuple(pl.BlockSpec(memory_space=pltpu.VMEM) for _ in outs),
        scratch_shapes=scratch,
        compiler_params=pltpu.CompilerParams(vmem_limit_bytes=16 * 2**20),
        cost_estimate=pl.CostEstimate(flops=flops, bytes_accessed=moved, transcendentals=0),
    )(place, *operands)


def shape(*dims, dtype=bf16):
    return jax.ShapeDtypeStruct(dims, dtype)


def text_kernel(place, cap, rows, z_out):
    text = fold(unit_rows(cap[...])[0].astype(bf16))
    piece = rows[:, pl.ds(pl.multiple_of(place[1] * 768, 384), 768)]
    for k in range(8):
        z_out[k, :48, :] = text
        z_out[k, 48:96, :] = piece[:, :384]
        z_out[k, 96:, :] = piece[:, 384:]


def weight_kernel(place, ids, pic, tokens, other_tokens, adj, other_adj, *rest):
    a0, a1, a2, a3, b_own, b_out, image, turned, both, block = rest
    y, low, c = place[0], place[2] == 0, place[3]
    line = lax.broadcasted_iota(jnp.int32, (16, 384), 0)
    number = jnp.zeros((16, 384), jnp.int32)
    for i in range(16):
        number = jnp.where(line == i, ids[i], number)
    lane = lax.broadcasted_iota(jnp.int32, (16, 384), 1)
    split = jnp.where(lane % 2 == 0, number >> 6, number & 63)
    image[48:, :] = split.astype(f32).astype(bf16)
    image[:48, :] = fold(unit_rows(pic[...])[0].astype(bf16))
    for source, first in ((tokens, 0), (other_tokens, 384)):
        turned[...] = source[...].T
        for chip in range(16):
            here = pl.ds(pl.multiple_of(chip * 96 + c * 48, 16), 48)
            both[chip * 48 : chip * 48 + 48, first : first + 384] = turned[here, :]
    for k, out in enumerate((a0, a1, a2, a3)):
        at = pl.ds(pl.multiple_of(((y - k) & 3) * 384, 384), 384)
        block[:384, :] = adj[:, at]
        block[384:, :] = other_adj[:, at]
        acc = jnp.dot(both[...], block[...], preferred_element_type=f32).astype(bf16)
        out[:CUT, :] = acc[:CUT]
        out[CUT : 2 * CUT, :] = acc[384 : 384 + CUT]
        b_own[:, at] = jnp.where(low, acc[CUT:384], acc[384 + CUT :])
        b_out[:, at] = jnp.where(low, acc[384 + CUT :], acc[CUT:384])
        if k:
            out[2 * CUT :, :] = image[...]


def first_sum_kernel(
    place, a0, a1, a2, a3, b_own, b_in, image, a_own, near, column, *rest
):
    b0, b1, b2, b3, total = rest
    y, xh = place[0], place[2]
    del total
    for first, out in ((xh, a_own), (1 - xh, near)):
        here = pl.ds(pl.multiple_of(first * CUT, 16), CUT)
        half = a0[here, :].astype(f32)
        for part in (a1, a2, a3):
            half = half + part[here, :].astype(f32)
        out[:CUT, :] = half.astype(out.dtype)
    for k, out in enumerate((b0, b1, b2, b3)):
        at = pl.ds(pl.multiple_of(((y - k) & 3) * 384, 384), 384)
        both = b_own[:, at].astype(f32) + b_in[:, at].astype(f32)
        out[...] = both.astype(out.dtype)
    lane = lax.broadcasted_iota(jnp.int32, (16, 384), 1)
    ids = image[48:, :].astype(f32)
    for k, part in enumerate((a1, a2, a3), 1):
        ids = jnp.where(lane // 2 == k, part[2 * CUT + 48 :, :].astype(f32), ids)
    for target, first in ((near, CUT), (column, 0)):
        target[first : first + 48, :] = image[:48, :]
        for k, part in enumerate((a1, a2, a3), 1):
            at = first + 48 * k
            target[at : at + 48, :] = part[2 * CUT : 2 * CUT + 48, :]
        target[first + 192 :, :] = ids.astype(bf16)


def tile_kernel(place, sharp, bias, i0, i1, i2, i3, other_text, along_z, a_own, *rest):
    b0, b1, b2, b3, rows, weight, g0, g1, g2, g3, t_own, t_out, images, texts, ids = rest
    for k in range(8):
        rows[k] = along_z[k, 48:, :]
    weight[:CUT, :] = (a_own[...] + i1[:CUT, :].astype(f32)).astype(bf16)
    total = b0[...]
    for part in (b1, b2, b3):
        total = total + part[...].astype(f32)
    weight[CUT:, :] = total.astype(bf16)
    y, xl, xh, c = place[0], place[1], place[2], place[3]
    for k, part in enumerate((i0, i1, i2, i3)):
        first = part.shape[0] - 208
        split = part[first + 192 :, :128].astype(f32)
        for j in range(4):
            at = k * 64 + j * 16
            here = first + j * 48
            images[at : at + 16, :] = unfold(part[here : here + 48, :])
            number = split[:, 2 * j : 2 * j + 1] * 64.0 + split[:, 2 * j + 1 : 2 * j + 2]
            ids[at : at + 16, :] = number.astype(jnp.int32)
    for k in range(8):
        texts[k * 16 : k * 16 + 16, :] = unfold(along_z[k, :48, :])
        texts[128 + k * 16 : 144 + k * 16, :] = unfold(other_text[k, :, :])
    sharpness, offset = sharp[0], bias[0]
    col = lax.broadcasted_iota(jnp.int32, (256, 256), 1)
    core = jnp.where(col < 128, c, 1 - c)
    first = ((xl * 4 + y) * 2 + xh) * 256
    index = first + (((col & 127) >> 4) * 2 + core) * 16 + (col & 15)
    dots = lax.dot_general(images[...], texts[...], BACK, preferred_element_type=f32)
    labels = (ids[...] == index).astype(f32)
    weights = sharpness * (jax.nn.sigmoid(sharpness * dots + offset) - labels)
    half = weights.astype(bf16)
    for k in range(4):
        part = jnp.dot(half[k * 64 : k * 64 + 64], texts[...], preferred_element_type=f32)
        for j, out in enumerate((g0, g1, g2, g3)):
            out[k * 48 : k * 48 + 48, :] = fold(part[j * 16 : j * 16 + 16]).astype(out.dtype)
    half = weights.T.astype(bf16)
    t_own[...] = jnp.dot(half[:128], images[...], preferred_element_type=f32)
    t_out[...] = jnp.dot(half[128:], images[...], preferred_element_type=f32).astype(bf16)


def send_back_kernel(place, t_own, t_in, weight, out):
    total = (t_own[...] + t_in[...].astype(f32)).astype(bf16)
    for k in range(8):
        out[k, :48, :] = fold(total[k * 16 : k * 16 + 16])
        out[k, 48:, :] = weight[k * 48 : k * 48 + 48, :]


def middle_kernel(place, back, cap, g0, g1, g2, g3, grad, pieces, h0, h1, h2, h3):
    total = back[0].astype(f32)
    for k in range(1, 8):
        total = total + back[k].astype(f32)
    grad[...] = back_through_norm(cap[...], unfold(total[:48]))
    piece = total[48:].astype(bf16)
    for k in range(8):
        pieces[k] = piece
    total = g0[...]
    for part in (g1, g2, g3):
        total = total + part[...].astype(f32)
    for k, out in enumerate((h0, h1, h2, h3)):
        out[...] = total[k * 48 : k * 48 + 48].astype(out.dtype)


def end_kernel(place, h0, h1, h2, h3, pic, pieces, image_grad, weight_grad):
    total = h0[...]
    for part in (h1, h2, h3):
        total = total + part[...].astype(f32)
    image_grad[...] = back_through_norm(pic[...], unfold(total))
    for k in range(4):
        piece = pieces[k].astype(f32) + pieces[4 + k].astype(f32)
        weight_grad[:, k * 384 : k * 384 + 384] = piece * (1.0 / math.sqrt(98304))


def project_kernel(place, adj, w, w_pair, other, other_pair, *rest):
    out, rows = rest[-2:]
    xl, c = place[1], place[3]
    for core, side, part in ((c, xl, w), (c, 1 - xl, w_pair), (1 - c, xl, other), (1 - c, 1 - xl, other_pair)):
        for k in range(2):
            at = pl.ds(pl.multiple_of(side * 768 + k * 384, 384), 384)
            for z in range(8):
                rows[z * 2 + core, :, at] = part[z, k * 48 : k * 48 + 48, :]
    for k in range(2):
        part = rows[k * 8 : k * 8 + 8].reshape(384, 1536)
        out[:, k * 384 : k * 384 + 384] = lax.dot_general(
            adj[...], part, BACK, preferred_element_type=f32
        ).astype(bf16)


def project(place, half, adj, parts, before=None):
    whole = pl.BlockSpec(memory_space=pltpu.VMEM)
    operands = [adj, *parts] + ([] if before is None else [before])
    in_specs = [whole] * 5 + ([] if before is None else [pl.BlockSpec(memory_space=pl.ANY)])
    return pl.pallas_call(
        project_kernel,
        grid_spec=pltpu.PrefetchScalarGridSpec(
            num_scalar_prefetch=1,
            grid=(1,),
            in_specs=in_specs,
            out_specs=pl.BlockSpec((384, 768), lambda i, place: (0, place[half])),
            scratch_shapes=[pltpu.VMEM((16, 48, 1536), bf16)],
        ),
        out_shape=shape(384, 1536),
        input_output_aliases={} if before is None else {6: 0},
        compiler_params=pltpu.CompilerParams(vmem_limit_bytes=16 * 2**20),
        cost_estimate=pl.CostEstimate(
            flops=2 * 384 * 768 * 1536, bytes_accessed=6 * 2**20, transcendentals=0
        ),
    )(place, *operands)


def per_device(
    picture_vectors_prenorm,
    caption_vectors_prenorm,
    matched_caption_ids,
    sharpness_coefficient,
    additive_offset_term,
    heads_mixed_concluding,
    dense_result_adjoint,
    dense_mapping_matrix,
):
    y, xl, xh, c = (lax.axis_index(name) for name in ("y", "xl", "xh", "c"))
    place = jnp.stack([y, xl, xh, c, 1 - xh]).astype(jnp.int32)
    other_adjoint = swap_cores(dense_result_adjoint)
    other_tokens = swap_cores(heads_mixed_concluding)

    (along_z,) = call(
        text_kernel, (shape(8, 144, 384),), place, caption_vectors_prenorm, dense_mapping_matrix
    )
    along_z = exchange(after(along_z, other_tokens), "z")

    *a, b_own, b_out, image = call(
        weight_kernel,
        (
            shape(2 * CUT, 384),
            *[shape(2 * CUT + 64, 384)] * 3,
            shape(384 - CUT, 1536),
            shape(384 - CUT, 1536),
            shape(64, 384),
        ),
        place,
        matched_caption_ids,
        picture_vectors_prenorm,
        heads_mixed_concluding,
        other_tokens,
        dense_result_adjoint,
        other_adjoint,
        scratch=[
            pltpu.VMEM((1536, 384), bf16),
            pltpu.VMEM((768, 768), bf16),
            pltpu.VMEM((768, 384), bf16),
        ],
        spaces=(pltpu.SMEM,),
        flops=4 * 768 * 384 * 1536,
    )
    b_in = swap_halves(b_out)
    a_in = [turn(a[k], COLUMN, -k) for k in (1, 2, 3)]
    a_own, near, column, *b = call(
        first_sum_kernel,
        (
            shape(CUT, 384, dtype=f32),
            shape(CUT + 208, 384),
            shape(208, 384),
            shape(384 - CUT, 384, dtype=f32),
            *[shape(384 - CUT, 384)] * 3,
        ),
        place,
        a[0],
        *a_in,
        b_own,
        b_in,
        image,
        scratch=[pltpu.VMEM((2 * CUT, 384), f32)],
    )
    near_in = swap_halves(near)
    b = [b[0]] + [turn(b[k], COLUMN, -k) for k in (1, 2, 3)]
    along_z = after(along_z, near)
    other_text = swap_cores(along_z[:, :48])
    sent = after(column, other_text)
    pair_in, far_in = swap_pairs(sent), swap_far(sent)
    here, weight_plane, *g, t_own, t_out = call(
        tile_kernel,
        (
            shape(8, 96, 384),
            shape(384, 384),
            shape(192, 384, dtype=f32),
            *[shape(192, 384)] * 3,
            shape(128, 1152, dtype=f32),
            shape(128, 1152),
        ),
        place,
        sharpness_coefficient,
        additive_offset_term,
        column,
        near_in,
        pair_in,
        far_in,
        other_text,
        along_z,
        a_own,
        *b,
        scratch=[
            pltpu.VMEM((256, 1152), bf16),
            pltpu.VMEM((256, 1152), bf16),
            pltpu.VMEM((256, 1), jnp.int32),
        ],
        spaces=(pltpu.SMEM, pltpu.SMEM),
        flops=6 * 256 * 256 * 1152,
    )

    pair = swap_pairs(here)
    there = swap_halves(here)
    there_pair = swap_pairs(there)

    t_in = swap_cores(t_out)
    (back,) = call(send_back_kernel, (shape(8, 96, 384),), place, t_own, t_in, weight_plane)
    other, other_pair = swap_cores(here), swap_cores(pair)
    back = exchange(back, "z")
    attn_grad = project(
        place, 2, dense_result_adjoint, (here, pair, other, other_pair)
    )

    g = [g[0]] + [turn(g[k], COLUMN, k) for k in (1, 2, 3)]
    text_grad, pieces, *h = call(
        middle_kernel,
        (
            shape(16, 1152, dtype=f32),
            shape(8, 48, 384),
            shape(48, 384, dtype=f32),
            *[shape(48, 384)] * 3,
        ),
        place,
        after(back, attn_grad),
        caption_vectors_prenorm,
        *g,
    )
    pieces = exchange(pieces, ("xl", "y"))
    h = [h[0], swap_halves(h[1]), swap_pairs(h[2]), swap_far(h[3])]
    attn_grad = project(
        place,
        4,
        dense_result_adjoint,
        (there_pair, there, swap_cores(after(there_pair, h[0])), swap_cores(after(there, h[0]))),
        attn_grad,
    )
    image_grad, weight_grad = call(
        end_kernel,
        (shape(16, 1152, dtype=f32), shape(48, 1536, dtype=f32)),
        place,
        *h,
        picture_vectors_prenorm,
        after(pieces, attn_grad),
    )
    return (image_grad, text_grad, attn_grad, weight_grad)


def solution(mesh):
    chips = Mesh(mesh.devices.reshape(SIZES), AXES)
    everywhere = P(AXES, None)
    by_group = P(("xh", "z", "c"), None)
    return jax.shard_map(
        per_device,
        mesh=chips,
        in_specs=(
            everywhere,
            everywhere,
            P(AXES),
            P(),
            P(),
            everywhere,
            everywhere,
            by_group,
        ),
        out_specs=(everywhere, everywhere, everywhere, by_group),
        check_vma=False,
    )
```

```python
import math

import jax
import jax.numpy as jnp
from jax import lax
from jax.experimental import pallas as pl
from jax.experimental.pallas import tpu as pltpu
from jax.sharding import Mesh, PartitionSpec as P

stability_floor = 1e-06
f32, bf16 = jnp.float32, jnp.bfloat16

AXES = ("xl", "y", "xh", "z", "c")
SIZES = (2, 4, 2, 8, 2)
ROW = (("xl", "xh"), (0, 2, 1, 3))
COLUMN = ("y", (0, 1, 2, 3))
CUT = 192
BACK = (((1,), (1,)), ((), ()))


def swap_cores(x):
    return lax.ppermute(x, "c", [(0, 1), (1, 0)])


def turn(x, ring, by):
    axes, at = ring
    return lax.ppermute(x, axes, [(at[i], at[(i + by) % 4]) for i in range(4)])


def swap_halves(x):
    axes, at = ROW
    return lax.ppermute(x, axes, [(at[i], at[3 - i]) for i in range(4)])


def swap_pairs(x):
    return lax.ppermute(x, "xl", [(0, 1), (1, 0)])


def swap_far(x):
    return lax.ppermute(x, "xh", [(0, 1), (1, 0)])


def exchange(x, axes):
    return lax.all_to_all(x, axes, 0, 0, tiled=True)


def after(x, *earlier):
    return lax.optimization_barrier((x, *earlier))[0]


def fold(x):
    return jnp.concatenate([x[:, i * 384 : (i + 1) * 384] for i in range(3)], axis=0)


def unfold(x):
    return jnp.concatenate([x[i * 16 : (i + 1) * 16] for i in range(3)], axis=1)


def unit_rows(raw):
    row_scale = lax.rsqrt(jnp.sum(raw * raw, axis=1, keepdims=True) + stability_floor)
    return raw * row_scale, row_scale


def back_through_norm(raw, row_grad):
    normed, row_scale = unit_rows(raw)
    along_unit = jnp.sum(normed * row_grad, axis=1, keepdims=True)
    return (row_grad - normed * along_unit) * row_scale


def call(kernel, outs, place, *operands, scratch=(), flops=0, spaces=()):
    moved = sum(math.prod(o.shape) * o.dtype.itemsize for o in (*outs, *operands))
    spaces = tuple(spaces) + (pltpu.VMEM,) * (len(operands) - len(spaces))
    return pl.pallas_call(
        kernel,
        out_shape=tuple(outs),
        in_specs=[pl.BlockSpec(memory_space=space) for space in (pltpu.SMEM, *spaces)],
        out_specs=tuple(pl.BlockSpec(memory_space=pltpu.VMEM) for _ in outs),
        scratch_shapes=scratch,
        compiler_params=pltpu.CompilerParams(vmem_limit_bytes=16 * 2**20),
        cost_estimate=pl.CostEstimate(flops=flops, bytes_accessed=moved, transcendentals=0),
    )(place, *operands)


def shape(*dims, dtype=bf16):
    return jax.ShapeDtypeStruct(dims, dtype)


def text_kernel(place, cap, rows, z_out):
    text = fold(unit_rows(cap[...])[0].astype(bf16))
    piece = rows[:, pl.ds(pl.multiple_of(place[1] * 768, 384), 768)]
    for k in range(8):
        z_out[k, :48, :] = text
        z_out[k, 48:96, :] = piece[:, :384]
        z_out[k, 96:, :] = piece[:, 384:]


def weight_kernel(place, ids, pic, tokens, other_tokens, adj, other_adj, *rest):
    a0, a1, a2, a3, b_own, b_out, image, turned, both, block = rest
    y, low, c = place[0], place[2] == 0, place[3]
    line = lax.broadcasted_iota(jnp.int32, (16, 384), 0)
    number = jnp.zeros((16, 384), jnp.int32)
    for i in range(16):
        number = jnp.where(line == i, ids[i], number)
    lane = lax.broadcasted_iota(jnp.int32, (16, 384), 1)
    split = jnp.where(lane % 2 == 0, number >> 6, number & 63)
    image[48:, :] = split.astype(f32).astype(bf16)
    image[:48, :] = fold(unit_rows(pic[...])[0].astype(bf16))
    for source, first in ((tokens, 0), (other_tokens, 384)):
        turned[...] = source[...].T
        for chip in range(16):
            here = pl.ds(pl.multiple_of(chip * 96 + c * 48, 16), 48)
            both[chip * 48 : chip * 48 + 48, first : first + 384] = turned[here, :]
    for k, out in enumerate((a0, a1, a2, a3)):
        at = pl.ds(pl.multiple_of(((y - k) & 3) * 384, 384), 384)
        block[:384, :] = adj[:, at]
        block[384:, :] = other_adj[:, at]
        acc = jnp.dot(both[...], block[...], preferred_element_type=f32).astype(bf16)
        out[:CUT, :] = acc[:CUT]
        out[CUT : 2 * CUT, :] = acc[384 : 384 + CUT]
        b_own[:, at] = jnp.where(low, acc[CUT:384], acc[384 + CUT :])
        b_out[:, at] = jnp.where(low, acc[384 + CUT :], acc[CUT:384])
        if k:
            out[2 * CUT :, :] = image[...]


def first_sum_kernel(
    place, a0, a1, a2, a3, b_own, b_in, image, a_own, near, column, *rest
):
    b0, b1, b2, b3, total = rest
    y, xh = place[0], place[2]
    del total
    for first, out in ((xh, a_own), (1 - xh, near)):
        here = pl.ds(pl.multiple_of(first * CUT, 16), CUT)
        half = a0[here, :].astype(f32)
        for part in (a1, a2, a3):
            half = half + part[here, :].astype(f32)
        out[:CUT, :] = half.astype(out.dtype)
    for k, out in enumerate((b0, b1, b2, b3)):
        at = pl.ds(pl.multiple_of(((y - k) & 3) * 384, 384), 384)
        both = b_own[:, at].astype(f32) + b_in[:, at].astype(f32)
        out[...] = both.astype(out.dtype)
    lane = lax.broadcasted_iota(jnp.int32, (16, 384), 1)
    ids = image[48:, :].astype(f32)
    for k, part in enumerate((a1, a2, a3), 1):
        ids = jnp.where(lane // 2 == k, part[2 * CUT + 48 :, :].astype(f32), ids)
    for target, first in ((near, CUT), (column, 0)):
        target[first : first + 48, :] = image[:48, :]
        for k, part in enumerate((a1, a2, a3), 1):
            at = first + 48 * k
            target[at : at + 48, :] = part[2 * CUT : 2 * CUT + 48, :]
        target[first + 192 :, :] = ids.astype(bf16)


def tile_kernel(place, sharp, bias, i0, i1, i2, i3, other_text, along_z, a_own, *rest):
    b0, b1, b2, b3, rows, weight, g0, g1, g2, g3, t_own, t_out, images, texts, ids = rest
    for k in range(8):
        rows[k] = along_z[k, 48:, :]
    weight[:CUT, :] = (a_own[...] + i1[:CUT, :].astype(f32)).astype(bf16)
    total = b0[...]
    for part in (b1, b2, b3):
        total = total + part[...].astype(f32)
    weight[CUT:, :] = total.astype(bf16)
    y, xl, xh, c = place[0], place[1], place[2], place[3]
    for k, part in enumerate((i0, i1, i2, i3)):
        first = part.shape[0] - 208
        split = part[first + 192 :, :128].astype(f32)
        for j in range(4):
            at = k * 64 + j * 16
            here = first + j * 48
            images[at : at + 16, :] = unfold(part[here : here + 48, :])
            number = split[:, 2 * j : 2 * j + 1] * 64.0 + split[:, 2 * j + 1 : 2 * j + 2]
            ids[at : at + 16, :] = number.astype(jnp.int32)
    for k in range(8):
        texts[k * 16 : k * 16 + 16, :] = unfold(along_z[k, :48, :])
        texts[128 + k * 16 : 144 + k * 16, :] = unfold(other_text[k, :, :])
    sharpness, offset = sharp[0], bias[0]
    col = lax.broadcasted_iota(jnp.int32, (256, 256), 1)
    core = jnp.where(col < 128, c, 1 - c)
    first = ((xl * 4 + y) * 2 + xh) * 256
    index = first + (((col & 127) >> 4) * 2 + core) * 16 + (col & 15)
    dots = lax.dot_general(images[...], texts[...], BACK, preferred_element_type=f32)
    labels = (ids[...] == index).astype(f32)
    weights = sharpness * (jax.nn.sigmoid(sharpness * dots + offset) - labels)
    half = weights.astype(bf16)
    part = jnp.dot(half, texts[...], preferred_element_type=f32)
    for k in range(4):
        for j, out in enumerate((g0, g1, g2, g3)):
            at = k * 64 + j * 16
            out[k * 48 : k * 48 + 48, :] = fold(part[at : at + 16]).astype(out.dtype)
    half = weights.T.astype(bf16)
    part = jnp.dot(half, images[...], preferred_element_type=f32)
    t_own[...] = part[:128]
    t_out[...] = part[128:].astype(bf16)


def send_back_kernel(place, t_own, t_in, weight, out):
    total = (t_own[...] + t_in[...].astype(f32)).astype(bf16)
    for k in range(8):
        out[k, :48, :] = fold(total[k * 16 : k * 16 + 16])
        out[k, 48:, :] = weight[k * 48 : k * 48 + 48, :]


def middle_kernel(place, back, cap, g0, g1, g2, g3, grad, pieces, h0, h1, h2, h3):
    total = back[0].astype(f32)
    for k in range(1, 8):
        total = total + back[k].astype(f32)
    grad[...] = back_through_norm(cap[...], unfold(total[:48]))
    piece = total[48:].astype(bf16)
    for k in range(8):
        pieces[k] = piece
    total = g0[...]
    for part in (g1, g2, g3):
        total = total + part[...].astype(f32)
    for k, out in enumerate((h0, h1, h2, h3)):
        out[...] = total[k * 48 : k * 48 + 48].astype(out.dtype)


def end_kernel(place, h0, h1, h2, h3, pic, pieces, image_grad, weight_grad):
    total = h0[...]
    for part in (h1, h2, h3):
        total = total + part[...].astype(f32)
    image_grad[...] = back_through_norm(pic[...], unfold(total))
    for k in range(4):
        piece = pieces[k].astype(f32) + pieces[4 + k].astype(f32)
        weight_grad[:, k * 384 : k * 384 + 384] = piece * (1.0 / math.sqrt(98304))


def project_kernel(place, adj, w, w_pair, other, other_pair, *rest):
    out, rows = rest[-2:]
    xl, c = place[1], place[3]
    for core, side, part in ((c, xl, w), (c, 1 - xl, w_pair), (1 - c, xl, other), (1 - c, 1 - xl, other_pair)):
        for k in range(2):
            at = pl.ds(pl.multiple_of(side * 768 + k * 384, 384), 384)
            for z in range(8):
                rows[z * 2 + core, :, at] = part[z, k * 48 : k * 48 + 48, :]
    part = rows[...].reshape(768, 1536)
    part = lax.dot_general(adj[...], part, BACK, preferred_element_type=f32)
    out[...] = part.astype(bf16)


def project(place, half, adj, parts, before=None):
    whole = pl.BlockSpec(memory_space=pltpu.VMEM)
    operands = [adj, *parts] + ([] if before is None else [before])
    in_specs = [whole] * 5 + ([] if before is None else [pl.BlockSpec(memory_space=pl.ANY)])
    return pl.pallas_call(
        project_kernel,
        grid_spec=pltpu.PrefetchScalarGridSpec(
            num_scalar_prefetch=1,
            grid=(1,),
            in_specs=in_specs,
            out_specs=pl.BlockSpec((384, 768), lambda i, place: (0, place[half])),
            scratch_shapes=[pltpu.VMEM((16, 48, 1536), bf16)],
        ),
        out_shape=shape(384, 1536),
        input_output_aliases={} if before is None else {6: 0},
        compiler_params=pltpu.CompilerParams(vmem_limit_bytes=16 * 2**20),
        cost_estimate=pl.CostEstimate(
            flops=2 * 384 * 768 * 1536, bytes_accessed=6 * 2**20, transcendentals=0
        ),
    )(place, *operands)


def per_device(
    picture_vectors_prenorm,
    caption_vectors_prenorm,
    matched_caption_ids,
    sharpness_coefficient,
    additive_offset_term,
    heads_mixed_concluding,
    dense_result_adjoint,
    dense_mapping_matrix,
):
    y, xl, xh, c = (lax.axis_index(name) for name in ("y", "xl", "xh", "c"))
    place = jnp.stack([y, xl, xh, c, 1 - xh]).astype(jnp.int32)
    other_adjoint = swap_cores(dense_result_adjoint)
    other_tokens = swap_cores(heads_mixed_concluding)

    (along_z,) = call(
        text_kernel, (shape(8, 144, 384),), place, caption_vectors_prenorm, dense_mapping_matrix
    )
    along_z = exchange(after(along_z, other_tokens), "z")

    *a, b_own, b_out, image = call(
        weight_kernel,
        (
            shape(2 * CUT, 384),
            *[shape(2 * CUT + 64, 384)] * 3,
            shape(384 - CUT, 1536),
            shape(384 - CUT, 1536),
            shape(64, 384),
        ),
        place,
        matched_caption_ids,
        picture_vectors_prenorm,
        heads_mixed_concluding,
        other_tokens,
        dense_result_adjoint,
        other_adjoint,
        scratch=[
            pltpu.VMEM((1536, 384), bf16),
            pltpu.VMEM((768, 768), bf16),
            pltpu.VMEM((768, 384), bf16),
        ],
        spaces=(pltpu.SMEM,),
        flops=4 * 768 * 384 * 1536,
    )
    b_in = swap_halves(b_out)
    a_in = [turn(a[k], COLUMN, -k) for k in (1, 2, 3)]
    a_own, near, column, *b = call(
        first_sum_kernel,
        (
            shape(CUT, 384, dtype=f32),
            shape(CUT + 208, 384),
            shape(208, 384),
            shape(384 - CUT, 384, dtype=f32),
            *[shape(384 - CUT, 384)] * 3,
        ),
        place,
        a[0],
        *a_in,
        b_own,
        b_in,
        image,
        scratch=[pltpu.VMEM((2 * CUT, 384), f32)],
    )
    near_in = swap_halves(near)
    b = [b[0]] + [turn(b[k], COLUMN, -k) for k in (1, 2, 3)]
    along_z = after(along_z, near)
    other_text = swap_cores(along_z[:, :48])
    sent = after(column, other_text)
    pair_in, far_in = swap_pairs(sent), swap_far(sent)
    here, weight_plane, *g, t_own, t_out = call(
        tile_kernel,
        (
            shape(8, 96, 384),
            shape(384, 384),
            shape(192, 384, dtype=f32),
            *[shape(192, 384)] * 3,
            shape(128, 1152, dtype=f32),
            shape(128, 1152),
        ),
        place,
        sharpness_coefficient,
        additive_offset_term,
        column,
        near_in,
        pair_in,
        far_in,
        other_text,
        along_z,
        a_own,
        *b,
        scratch=[
            pltpu.VMEM((256, 1152), bf16),
            pltpu.VMEM((256, 1152), bf16),
            pltpu.VMEM((256, 1), jnp.int32),
        ],
        spaces=(pltpu.SMEM, pltpu.SMEM),
        flops=6 * 256 * 256 * 1152,
    )

    pair = swap_pairs(here)
    there = swap_halves(here)
    there_pair = swap_pairs(there)

    t_in = swap_cores(t_out)
    (back,) = call(send_back_kernel, (shape(8, 96, 384),), place, t_own, t_in, weight_plane)
    other, other_pair = swap_cores(here), swap_cores(pair)
    back = exchange(back, "z")
    attn_grad = project(
        place, 2, dense_result_adjoint, (here, pair, other, other_pair)
    )

    g = [g[0]] + [turn(g[k], COLUMN, k) for k in (1, 2, 3)]
    text_grad, pieces, *h = call(
        middle_kernel,
        (
            shape(16, 1152, dtype=f32),
            shape(8, 48, 384),
            shape(48, 384, dtype=f32),
            *[shape(48, 384)] * 3,
        ),
        place,
        after(back, attn_grad),
        caption_vectors_prenorm,
        *g,
    )
    pieces = exchange(pieces, ("xl", "y"))
    h = [h[0], swap_halves(h[1]), swap_pairs(h[2]), swap_far(h[3])]
    attn_grad = project(
        place,
        4,
        dense_result_adjoint,
        (there_pair, there, swap_cores(after(there_pair, h[0])), swap_cores(after(there, h[0]))),
        attn_grad,
    )
    image_grad, weight_grad = call(
        end_kernel,
        (shape(16, 1152, dtype=f32), shape(48, 1536, dtype=f32)),
        place,
        *h,
        picture_vectors_prenorm,
        after(pieces, attn_grad),
    )
    return (image_grad, text_grad, attn_grad, weight_grad)


def solution(mesh):
    chips = Mesh(mesh.devices.reshape(SIZES), AXES)
    everywhere = P(AXES, None)
    by_group = P(("xh", "z", "c"), None)
    return jax.shard_map(
        per_device,
        mesh=chips,
        in_specs=(
            everywhere,
            everywhere,
            P(AXES),
            P(),
            P(),
            everywhere,
            everywhere,
            by_group,
        ),
        out_specs=(everywhere, everywhere, everywhere, by_group),
        check_vma=False,
    )
```
